32 devices in a mesh: group: 4 (over z), dev: 8 (over y, x, core).
Axes of the slice: x: 2, y: 2, z: 4, core: 2. Of those that a mesh axis runs over, the one named last changes fastest.
Arguments:
- blocks_in: float32 [992, 8, 4096], P(('group', 'dev')), as said below
- counts: int32 [32], P(('group', 'dev')), may hold values from 1 to 31, as said below
Outputs:
- blocks_out: float32 [512, 8, 4096], P(('group', 'dev'))
The draws below stay inside these ranges and needn't reach their ends.
Inputs may be any that keep to these rules, and one draw needn't show every extreme that they name: `blocks_in`: every slot holds a state of positive density and pressure. Device i (in the order of group+dev) holds its live meshblocks in its first counts[i] slots, in curve order. The counts sum to 512; for every device i, starts[i] - i * 16 lies in 0 .. 15.
All inputs are finite; a program needn't handle non-finite values.
Results may differ from the reference program's by a relative error of at most 0.0003.
Values sent between devices are 32-bit elements; how exact they have to be, the bound alone decides.
A program may use at most 192 MiB of HBM per device.

```python
import math
import jax
import jax.numpy as jnp
from jax import lax

BS = 16
BRICK_Y = 2
BRICK_Z = 8
BRICK_X = 1
BLK_DEV = 16
FIELDS = 8
DEVS = 32
CAP = 31
BLOCKS = 512
N_GROUP = 4
N_DEV = 8


GAMMA = 5.0 / 3.0


def draw_counts(key, part):
    key = jax.random.fold_in(key, 1)
    key_offsets, key_place = jax.random.split(key)
    surplus = jax.random.randint(key_offsets, (DEVS + 1,), 0, BLK_DEV).astype(jnp.int32)
    surplus = surplus.at[0].set(0).at[DEVS].set(0)
    chosen = jax.random.randint(key_place, (), 0, DEVS - 2).astype(jnp.int32)
    surplus = surplus.at[chosen].set(0).at[chosen + 1].set(BLK_DEV - 1)
    surplus = surplus.at[DEVS - 1].set(BLK_DEV - 1)
    return (BLK_DEV + surplus[1:] - surplus[:-1]).astype(jnp.int32)


def draw_blocks_in(key, part):
    key = jax.random.fold_in(key, 2)
    keys = jax.random.split(key, 6)
    slots = DEVS * CAP
    cells = BS * BS * BS
    amplitude = jnp.exp(jax.random.uniform(keys[0], (slots, 1, 1), jnp.float32, math.log(0.3), math.log(3.0)))
    motion = jnp.clip(jax.random.normal(keys[1], (slots, 3, cells), jnp.float32), -3.0, 3.0)
    field_noise = jnp.clip(jax.random.normal(keys[2], (slots, 3, cells), jnp.float32), -3.0, 3.0)
    velocity = 0.4 * amplitude * motion
    magnetic = 0.4 * amplitude * field_noise
    density = jax.random.uniform(keys[3], (slots, 1, cells), jnp.float32, 0.5, 1.5)
    pressure = jax.random.uniform(keys[4], (slots, 1, cells), jnp.float32, 0.6, 1.4)
    energy = pressure / (GAMMA - 1.0) + 0.5 * density * jnp.sum(velocity * velocity, axis=1, keepdims=True) + 0.5 * jnp.sum(magnetic * magnetic, axis=1, keepdims=True)
    return jnp.concatenate([density, density * velocity, energy, magnetic], axis=1).astype(jnp.float32)


def setup_inputs(seed: int = 0) -> dict:
    splits = jax.random.split(jax.random.key(seed), 3)
    blocks_in = draw_blocks_in(jax.random.fold_in(splits[2], 71), 0)
    counts = draw_counts(jax.random.fold_in(splits[2], 71), 0)
    return {"blocks_in": blocks_in, "counts": counts}


GAMMA = 5.0 / 3.0
COURANT = 0.25
DENSITY_FLOOR = 0.05
PRESSURE_FLOOR = 0.05

def trimmed(values, along, front, back):
    return lax.slice_in_dim(values, front, values.shape[along] - back, axis=along)

def primitive(state):
    density = jnp.maximum(state[0], DENSITY_FLOOR)
    velocity = state[1:4] / density
    magnetic = state[5:8]
    kinetic = 0.5 * density * lax.optimization_barrier(jnp.sum(velocity * velocity, axis=0))
    magnetic_energy = 0.5 * lax.optimization_barrier(jnp.sum(magnetic * magnetic, axis=0))
    pressure = jnp.maximum((GAMMA - 1.0) * (state[4] - kinetic - magnetic_energy), PRESSURE_FLOOR)
    return jnp.concatenate([density[None], velocity, pressure[None], magnetic], axis=0)

def conserved(prims):
    density = prims[0]
    velocity = prims[1:4]
    magnetic = prims[5:8]
    energy = prims[4] / (GAMMA - 1.0) + 0.5 * density * lax.optimization_barrier(jnp.sum(velocity * velocity, axis=0)) + 0.5 * lax.optimization_barrier(jnp.sum(magnetic * magnetic, axis=0))
    return jnp.concatenate([density[None], density * velocity, energy[None], magnetic], axis=0)

def fast_speed(prims, normal):
    density = prims[0]
    sound = GAMMA * prims[4] / density
    alfven = lax.optimization_barrier(jnp.sum(prims[5:8] * prims[5:8], axis=0)) / density
    along_field = prims[5 + normal] * prims[5 + normal] / density
    total = sound + alfven
    root = jnp.sqrt(jnp.maximum(total * total - 4.0 * sound * along_field, 0.0))
    return jnp.sqrt(0.5 * (total + root))

def physical_flux(prims, state, normal):
    density = prims[0]
    velocity = prims[1:4]
    magnetic = prims[5:8]
    speed_normal = velocity[normal]
    field_normal = magnetic[normal]
    total_pressure = prims[4] + 0.5 * lax.optimization_barrier(jnp.sum(magnetic * magnetic, axis=0))
    unit_normal = jnp.array([1.0 if component == normal else 0.0 for component in range(3)], dtype=jnp.float32)
    unit_normal = unit_normal.reshape((3,) + (1,) * (velocity.ndim - 1))
    momentum_flux = density * velocity * speed_normal - magnetic * field_normal + unit_normal * total_pressure
    energy_flux = (state[4] + total_pressure) * speed_normal - field_normal * lax.optimization_barrier(jnp.sum(velocity * magnetic, axis=0))
    induction = speed_normal * magnetic - velocity * field_normal
    return jnp.concatenate([(density * speed_normal)[None], momentum_flux, energy_flux[None], induction], axis=0)

def hlle_flux(left, right, normal):
    state_left = conserved(left)
    state_right = conserved(right)
    flux_left = physical_flux(left, state_left, normal)
    flux_right = physical_flux(right, state_right, normal)
    fast_left = fast_speed(left, normal)
    fast_right = fast_speed(right, normal)
    upper = jnp.maximum(jnp.maximum(right[1 + normal] + fast_right, left[1 + normal] + fast_left), 0.0)
    lower = jnp.minimum(jnp.minimum(left[1 + normal] - fast_left, right[1 + normal] - fast_right), 0.0)
    return (upper * flux_left - lower * flux_right + upper * lower * (state_right - state_left)) / (upper - lower)

def minmod(first, second):
    return 0.5 * (jnp.sign(first) + jnp.sign(second)) * jnp.minimum(jnp.abs(first), jnp.abs(second))

def divergence(prims, along, normal):
    backward = trimmed(prims, along, 1, 1) - trimmed(prims, along, 0, 2)
    forward = trimmed(prims, along, 2, 0) - trimmed(prims, along, 1, 1)
    slope = minmod(backward, forward)
    left = trimmed(prims, along, 1, 2) + 0.5 * trimmed(slope, along, 0, 1)
    right = trimmed(prims, along, 2, 1) - 0.5 * trimmed(slope, along, 1, 0)
    flux = hlle_flux(left, right, normal)
    return trimmed(flux, along, 1, 0) - trimmed(flux, along, 0, 1)

def tendency(padded):
    prims = primitive(padded)
    across_x = trimmed(divergence(prims, 1, 0), 2, 2, 2)
    across_y = trimmed(divergence(prims, 2, 1), 1, 2, 2)
    wrapped = jnp.concatenate([prims[..., -2:], prims, prims[..., :2]], axis=3)
    across_z = trimmed(trimmed(divergence(wrapped, 3, 2), 1, 2, 2), 2, 2, 2)
    return -(across_x + across_y + across_z)

def signal_speed(state):
    prims = primitive(state)
    fastest = jnp.abs(prims[1]) + fast_speed(prims, 0)
    fastest = jnp.maximum(fastest, jnp.abs(prims[2]) + fast_speed(prims, 1))
    return jnp.maximum(fastest, jnp.abs(prims[3]) + fast_speed(prims, 2))

def whole_tendency(grid):
    padded = jnp.pad(grid, ((0, 0), (2, 2), (2, 2), (0, 0)), mode='wrap')
    width_x = BRICK_X * BS
    width_y = BRICK_Y * BS
    depth = grid.shape[3]

    def one_brick(index):
        group_index = (index // N_DEV).astype(jnp.int32)
        dev_index = (index % N_DEV).astype(jnp.int32)
        anchor = (jnp.zeros((), jnp.int32), (group_index * width_x).astype(jnp.int32), (dev_index * width_y).astype(jnp.int32), jnp.zeros((), jnp.int32))
        piece = lax.dynamic_slice(padded, anchor, (FIELDS, width_x + 4, width_y + 4, depth))
        return tendency(piece)
    bricks = lax.map(one_brick, jnp.arange(DEVS, dtype=jnp.int32))
    bricks = bricks.reshape(N_GROUP, N_DEV, FIELDS, width_x, width_y, depth)
    return jnp.transpose(bricks, (2, 0, 3, 1, 4, 5)).reshape(grid.shape)

def reference(blocks_in, counts):
    starts = (jnp.cumsum(counts) - counts).astype(jnp.int32)
    curve = jnp.arange(BLOCKS, dtype=jnp.int32)
    owner = (lax.optimization_barrier(jnp.sum((starts[None, :] <= curve[:, None]).astype(jnp.int32), axis=1)) - 1).astype(jnp.int32)
    slot_index = (curve - starts[owner]).astype(jnp.int32)
    live = blocks_in[owner * CAP + slot_index]
    grid = live.reshape(N_GROUP, N_DEV, BRICK_X, BRICK_Y, BRICK_Z, FIELDS, BS, BS, BS)
    grid = jnp.transpose(grid, (5, 0, 2, 6, 1, 3, 7, 4, 8)).reshape(FIELDS, N_GROUP * BRICK_X * BS, N_DEV * BRICK_Y * BS, BRICK_Z * BS)
    step = COURANT / jnp.max(signal_speed(grid))
    first = grid + step * whole_tendency(grid)
    second = 0.5 * (grid + first + step * whole_tendency(first))
    result = second.reshape(FIELDS, N_GROUP, BRICK_X, BS, N_DEV, BRICK_Y, BS, BRICK_Z, BS)
    return jnp.transpose(result, (1, 4, 2, 5, 7, 0, 3, 6, 8)).reshape(BLOCKS, FIELDS, BS * BS * BS)
```

```python
import functools

import jax
import jax.numpy as jnp
from jax import lax
from jax.experimental import pallas as pl
from jax.experimental.pallas import tpu as pltpu
from jax.sharding import PartitionSpec as P

BS = 16
BRICK_Y = 2
BRICK_Z = 8
BLK_DEV = 16
FIELDS = 8
LANES = 128
CHUNKS = 32
ROWS = CHUNKS * FIELDS
YV = 4

GAMMA = 5.0 / 3.0
COURANT = 0.25
DENSITY_FLOOR = 0.05
PRESSURE_FLOOR = 0.05
TINY = 1.2e-38

MESH = pl.DeviceIdType.MESH


def primitive(u):
    density = jnp.maximum(u[0], DENSITY_FLOOR)
    inverse = 1.0 / density
    vx, vy, vz = u[1] * inverse, u[2] * inverse, u[3] * inverse
    kinetic = 0.5 * density * (vx * vx + vy * vy + vz * vz)
    energy_b = 0.5 * (u[5] * u[5] + u[6] * u[6] + u[7] * u[7])
    pressure = jnp.maximum((GAMMA - 1.0) * (u[4] - kinetic - energy_b), PRESSURE_FLOOR)
    return [density, vx, vy, vz, pressure, u[5], u[6], u[7]], inverse


def fast_from(sound, alfven, along):
    total = sound + alfven
    inner = jnp.maximum(total * total - 4.0 * sound * along, TINY)
    outer = 0.5 * (total + inner * lax.rsqrt(inner))
    return outer * lax.rsqrt(outer)


def side(w, n):
    r, v, p, b = w[0], w[1:4], w[4], w[5:8]
    inverse = 1.0 / r
    b2 = b[0] * b[0] + b[1] * b[1] + b[2] * b[2]
    v2 = v[0] * v[0] + v[1] * v[1] + v[2] * v[2]
    half_b2 = 0.5 * b2
    m = [r * v[0], r * v[1], r * v[2]]
    energy = p * (1.0 / (GAMMA - 1.0)) + 0.5 * r * v2 + half_b2
    total_p = p + half_b2
    vn, bn = v[n], b[n]
    fast = fast_from(GAMMA * p * inverse, b2 * inverse, bn * bn * inverse)
    vb = v[0] * b[0] + v[1] * b[1] + v[2] * b[2]
    fm = [m[i] * vn - b[i] * bn for i in range(3)]
    fm[n] = fm[n] + total_p
    fe = (energy + total_p) * vn - bn * vb
    fb = [None if i == n else vn * b[i] - v[i] * bn for i in range(3)]
    return [r] + m + [energy] + b, [m[n]] + fm + [fe] + fb, vn, fast


def hlle(left, right, n):
    ul, fl, vl, cl = side(left, n)
    ur, fr, vr, cr = side(right, n)
    upper = jnp.maximum(jnp.maximum(vr + cr, vl + cl), 0.0)
    lower = jnp.minimum(jnp.minimum(vl - cl, vr - cr), 0.0)
    inverse = 1.0 / (upper - lower)
    a = upper * inverse
    b = lower * inverse
    c = a * lower
    out = []
    for f in range(FIELDS):
        jump = c * (ur[f] - ul[f])
        out.append(jump if fl[f] is None else a * fl[f] - b * fr[f] + jump)
    return out


def half_minmod(a, b):
    return 0.5 * (jnp.maximum(jnp.minimum(a, b), 0.0) + jnp.minimum(jnp.maximum(a, b), 0.0))


def roll(x, shift, axis):
    size = x.shape[axis]
    shift = shift % size
    return x if shift == 0 else pltpu.roll(x, shift, axis)


def lane_index():
    return lax.broadcasted_iota(jnp.int32, (8, LANES), 1)


def z_up(x, last):
    return jnp.where(last, roll(roll(x, 15, 1), -1, 0), roll(x, -1, 1))


def z_down(x, first):
    return jnp.where(first, roll(roll(x, -15, 1), 1, 0), roll(x, 1, 1))


def fill_primitives(u_ref, xlo_ref, xhi_ref, glo_ref, ghi_ref, w_ref):
    def planes(source, base):
        def one(c, carry):
            for v in range(YV):
                w, _ = primitive([source[c, f, v] for f in range(FIELDS)])
                for f in range(FIELDS):
                    w_ref[base + c, f, v + 1] = w[f]
            return carry

        lax.fori_loop(0, source.shape[0], one, 0)

    planes(xlo_ref, 0)
    planes(u_ref, 2)
    planes(xhi_ref, 2 + BS)

    def ghosts(c, carry):
        for ghost, v, base in ((glo_ref, 0, 96), (ghi_ref, YV + 1, 0)):
            u = [roll(ghost[c, f // 4], base - 32 * (f % 4), 1) for f in range(FIELDS)]
            w, _ = primitive(u)
            for f in range(FIELDS):
                w_ref[c + 2, f, v] = w[f]
        return carry

    lax.fori_loop(0, BS, ghosts, 0)


def x_faces(w_ref, fx_ref):
    for v in range(YV):
        def one(face, slope):
            left, right, after = [], [], []
            for f in range(FIELDS):
                here = w_ref[face + 1, f, v + 1]
                there = w_ref[face + 2, f, v + 1]
                beyond = w_ref[face + 3, f, v + 1]
                new = half_minmod(there - here, beyond - there)
                left.append(here + slope[f])
                right.append(there - new)
                after.append(new)
            flux = hlle(left, right, 0)
            for f in range(FIELDS):
                fx_ref[face, f, v] = flux[f]
            return tuple(after)

        first = tuple(
            half_minmod(
                w_ref[1, f, v + 1] - w_ref[0, f, v + 1], w_ref[2, f, v + 1] - w_ref[1, f, v + 1]
            )
            for f in range(FIELDS)
        )
        lax.fori_loop(0, BS + 1, one, first)


def y_faces(w_ref, c, f_ref):
    lane = lane_index()
    top = lane >= LANES - BS
    bottom = lane < BS
    left = [[None] * FIELDS for _ in range(YV + 1)]
    right = [[None] * FIELDS for _ in range(YV + 1)]
    for f in range(FIELDS):
        w = [w_ref[c + 2, f, v] for v in range(YV + 2)]
        rolled = [roll(x, -BS, 1) for x in w]
        up = [jnp.where(top, rolled[min(v + 1, YV + 1)], rolled[v]) for v in range(YV + 2)]
        diff = [up[v] - w[v] for v in range(YV + 2)]
        rolled = [roll(x, BS, 1) for x in diff]
        down = [jnp.where(bottom, rolled[max(v - 1, 0)], rolled[v]) for v in range(YV + 2)]
        slope = [half_minmod(down[v], diff[v]) for v in range(YV + 2)]
        low = [roll(w[v] - slope[v], -BS, 1) for v in range(YV + 2)]
        for v in range(YV + 1):
            left[v][f] = w[v] + slope[v]
            right[v][f] = jnp.where(top, low[v + 1], low[v])
    for v in range(YV + 1):
        flux = hlle(left[v], right[v], 1)
        for f in range(FIELDS):
            f_ref[f, v] = flux[f]


def tile_tendency(w_ref, fx_ref, fy_ref, c, v):
    lane = lane_index()
    bottom = lane < BS
    cz = lane % BS
    last, start = cz == BS - 1, cz == 0
    left, right = [], []
    for f in range(FIELDS):
        w = w_ref[c + 2, f, v + 1]
        diff = z_up(w, last) - w
        slope = half_minmod(z_down(diff, start), diff)
        left.append(w + slope)
        right.append(z_up(w - slope, last))
    flux = hlle(left, right, 2)
    out = []
    for f in range(FIELDS):
        across_z = flux[f] - z_down(flux[f], start)
        upper = fy_ref[f, v + 1]
        across_y = upper - jnp.where(bottom, roll(fy_ref[f, v], BS, 1), roll(upper, BS, 1))
        across_x = fx_ref[c + 1, f, v] - fx_ref[c, f, v]
        out.append(across_x + across_y + across_z)
    return out


def pack(tiles, base):
    group = lane_index() // 32
    out = []
    for q in range(2):
        total = roll(tiles[4 * q], -base, 1)
        for k in range(1, 4):
            total = jnp.where(group == k, roll(tiles[4 * q + k], 32 * k - base, 1), total)
        out.append(total)
    return out


def first_kernel(step_ref, u_ref, xlo, xhi, glo, ghi, out_ref, plo_ref, phi_ref, w_ref, fx_ref, fy_ref):
    fill_primitives(u_ref, xlo, xhi, glo, ghi, w_ref)
    x_faces(w_ref, fx_ref)

    def one(c, carry):
        step = step_ref[...]
        y_faces(w_ref, c, fy_ref)
        for v in range(YV):
            change = tile_tendency(w_ref, fx_ref, fy_ref, c, v)
            new = [u_ref[c, f, v] - step * change[f] for f in range(FIELDS)]
            for f in range(FIELDS):
                out_ref[c, f, v] = new[f]
            if v == 0:
                for q, tile in enumerate(pack(new, 0)):
                    plo_ref[c, q] = tile
            if v == YV - 1:
                for q, tile in enumerate(pack(new, 96)):
                    phi_ref[c, q] = tile
        return carry

    lax.fori_loop(0, BS, one, 0)


def second_kernel(step_ref, u_ref, one_ref, xlo, xhi, glo, ghi, out_ref, w_ref, fx_ref, fy_ref):
    fill_primitives(one_ref, xlo, xhi, glo, ghi, w_ref)
    x_faces(w_ref, fx_ref)

    def one(c, carry):
        step = step_ref[...]
        y_faces(w_ref, c, fy_ref)
        for v in range(YV):
            change = tile_tendency(w_ref, fx_ref, fy_ref, c, v)
            for f in range(FIELDS):
                new = 0.5 * (u_ref[c, f, v] + one_ref[c, f, v] - step * change[f])
                row = (v // 2) * (BRICK_Z * ROWS) + (c * 2 + v % 2) * FIELDS + f
                out_ref[pl.ds(row, BRICK_Z, stride=ROWS), :] = new
        return carry

    lax.fori_loop(0, BS, one, 0)


def ring(groups, devs):
    g, j = lax.axis_index("group"), lax.axis_index("dev")
    me = g * devs + j
    count = groups * devs
    after, before = lax.rem(me + 1, count), lax.rem(me + count - 1, count)
    curve_next = (after // devs, lax.rem(after, devs))
    curve_prev = (before // devs, lax.rem(before, devs))
    row = [(g, lax.rem(j + d, devs)) for d in range(1, devs)]
    column = [(lax.rem(g + d, groups), j) for d in range(1, groups)]
    return g, j, me, curve_next, curve_prev, row, column


def greet(peers):
    barrier = pltpu.get_barrier_semaphore()
    for peer in peers:
        pl.semaphore_signal(barrier, inc=1, device_id=peer, device_id_type=MESH)
    pl.semaphore_wait(barrier, len(peers))


def remote(source, target, send, recv, device):
    return pltpu.make_async_remote_copy(
        src_ref=source, dst_ref=target, send_sem=send, recv_sem=recv,
        device_id=device, device_id_type=MESH,
    )


def spread(source, slots, send, recv, peers):
    copies = [remote(source, slots.at[d], send.at[d], recv.at[d], p) for d, p in enumerate(peers)]
    for copy in copies:
        copy.start()
    for copy in copies:
        copy.wait()


def halo(g, j, groups, devs, u_ref, plo_ref, phi_ref, xlo, xhi, glo, ghi, send, recv):
    up = (lax.rem(g + 1, groups), j)
    down = (lax.rem(g + groups - 1, groups), j)
    right = (g, lax.rem(j + 1, devs))
    left = (g, lax.rem(j + devs - 1, devs))
    copies = [
        remote(u_ref.at[pl.ds(BS - 2, 2)], xlo, send.at[0], recv.at[0], up),
        remote(u_ref.at[pl.ds(0, 2)], xhi, send.at[1], recv.at[1], down),
        remote(phi_ref, glo, send.at[2], recv.at[2], right),
        remote(plo_ref, ghi, send.at[3], recv.at[3], left),
    ]
    for copy in copies:
        copy.start()
    for copy in copies:
        copy.wait()


def halo_kernel(groups, devs, u_ref, plo_ref, phi_ref, xlo, xhi, glo, ghi, send, recv):
    g, j = lax.axis_index("group"), lax.axis_index("dev")
    greet([
        (lax.rem(g + 1, groups), j),
        (lax.rem(g + groups - 1, groups), j),
        (g, lax.rem(j + 1, devs)),
        (g, lax.rem(j + devs - 1, devs)),
    ])
    halo(g, j, groups, devs, u_ref, plo_ref, phi_ref, xlo, xhi, glo, ghi, send, recv)


def signal_speed(u):
    w, inverse = primitive(u)
    b2 = [w[5 + i] * w[5 + i] for i in range(3)]
    sound = GAMMA * w[4] * inverse
    alfven = (b2[0] + b2[1] + b2[2]) * inverse
    speeds = [jnp.abs(w[1 + i]) + fast_from(sound, alfven, b2[i] * inverse) for i in range(3)]
    return jnp.maximum(jnp.maximum(speeds[0], speeds[1]), speeds[2])


def stage_kernel(count_ref, own_ref, out_ref, sem):
    copies = []
    for m in range(BLK_DEV - 1):
        base = jnp.maximum(count_ref[0] - BLK_DEV + 1 + m, 0) * ROWS
        copies.append(pltpu.make_async_copy(
            own_ref.at[pl.ds(pl.multiple_of(base, ROWS), ROWS)],
            out_ref.at[pl.ds(m * ROWS, ROWS)],
            sem.at[m],
        ))
    for copy in copies:
        copy.start()
    for copy in copies:
        copy.wait()


def gather_kernel(
    groups, devs, cap, count_ref, outgoing, own_ref,
    step_ref, small_ref, joined,
    count_msg, count_row, count_col, speed_msg, speed_row, speed_col,
    total_ref, block_sem, row_send, row_recv, col_send, col_recv,
    srow_send, srow_recv, scol_send, scol_recv, local_sem,
):
    g, j, me, curve_next, curve_prev, row, column = ring(groups, devs)
    greet(row + column + [curve_next, curve_prev])
    count = count_ref[0]
    blocks = remote(
        outgoing, joined.at[pl.ds(ROWS, (BLK_DEV - 1) * ROWS)], block_sem.at[0], block_sem.at[1],
        curve_next,
    )
    blocks.start()
    local = pltpu.make_async_copy(
        own_ref.at[pl.ds(0, BLK_DEV * ROWS)], joined.at[pl.ds(BLK_DEV * ROWS, BLK_DEV * ROWS)],
        local_sem.at[0],
    )
    local.start()

    count_msg[...] = jnp.full((8, LANES), count, jnp.int32)
    spread(count_msg, count_row, row_send, row_recv, row)
    before = jnp.zeros((8, LANES), jnp.int32)
    every = count_msg[...]
    for d in range(1, devs):
        value = count_row[d - 1]
        every = every + value
        before = before + jnp.where(d <= j, value, 0)
    count_msg[...] = every
    spread(count_msg, count_col, col_send, col_recv, column)
    for d in range(1, groups):
        before = before + jnp.where(d <= g, count_col[d - 1], 0)
    total_ref[...] = before - me * BLK_DEV
    narrow = pltpu.make_async_copy(total_ref, small_ref, local_sem.at[1])
    narrow.start()

    slot = lax.broadcasted_iota(jnp.int32, (8, LANES), 0)

    def chunk(t, top):
        for first in list(range(0, cap - 8, 8)) + [cap - 8]:
            u = [
                own_ref[pl.ds(first * ROWS + t * FIELDS + f, 8, stride=ROWS), :]
                for f in range(FIELDS)
            ]
            top = jnp.maximum(top, jnp.where(slot + first < count, signal_speed(u), 0.0))
        return top

    top = lax.fori_loop(0, CHUNKS, chunk, jnp.zeros((8, LANES), jnp.float32))
    speed_msg[...] = top
    spread(speed_msg, speed_row, srow_send, srow_recv, row)
    for d in range(devs - 1):
        top = jnp.maximum(top, speed_row[d])
    speed_msg[...] = top
    spread(speed_msg, speed_col, scol_send, scol_recv, column)
    for d in range(groups - 1):
        top = jnp.maximum(top, speed_col[d])
    top = jnp.max(jnp.max(top, axis=1, keepdims=True), axis=0, keepdims=True)
    step_ref[...] = COURANT / jnp.broadcast_to(top, (8, LANES))

    narrow.wait()
    local.wait()
    blocks.wait()


def assemble_kernel(small_ref, joined, u_ref, plo, phi):
    surplus = small_ref[0, 0]

    def assemble(c, carry):
        for v in range(YV):
            for f in range(FIELDS):
                base = (BLK_DEV - surplus + (v // 2) * BRICK_Z) * ROWS
                u_ref[c, f, v] = joined[
                    pl.ds(base + (c * 2 + v % 2) * FIELDS + f, BRICK_Z, stride=ROWS), :
                ]
        for q, tile in enumerate(pack([u_ref[c, f, 0] for f in range(FIELDS)], 0)):
            plo[c, q] = tile
        for q, tile in enumerate(pack([u_ref[c, f, YV - 1] for f in range(FIELDS)], 96)):
            phi[c, q] = tile
        return carry

    lax.fori_loop(0, BS, assemble, 0)


TILE = (8, LANES)
SLAB = (BS, FIELDS, YV) + TILE
EDGE = (2, FIELDS, YV) + TILE
PACK = (BS, 2) + TILE
LIMIT = 48 * 1024 * 1024


def f32(*shape):
    return jax.ShapeDtypeStruct(shape, jnp.float32)


VMEM = pl.BlockSpec(memory_space=pltpu.VMEM)
ANY = pl.BlockSpec(memory_space=pl.ANY)
SMEM = pl.BlockSpec(memory_space=pltpu.SMEM)


def body(groups, devs, blocks_in, counts):
    cap = blocks_in.shape[0]
    rows = blocks_in.reshape(cap, FIELDS, CHUNKS, LANES).transpose(0, 2, 1, 3)
    rows = rows.reshape(cap * ROWS, LANES)
    ghosts = (f32(*EDGE), f32(*EDGE), f32(*PACK), f32(*PACK))
    dma = pltpu.SemaphoreType.DMA
    plain = pltpu.CompilerParams(vmem_limit_bytes=LIMIT)
    outgoing = pl.pallas_call(
        stage_kernel,
        out_shape=f32((BLK_DEV - 1) * ROWS, LANES),
        in_specs=[SMEM, ANY],
        out_specs=VMEM,
        scratch_shapes=[dma((BLK_DEV - 1,))],
        compiler_params=plain,
        name="stage",
    )(counts, rows)
    step, small, joined = pl.pallas_call(
        functools.partial(gather_kernel, groups, devs, cap),
        out_shape=(
            f32(*TILE), jax.ShapeDtypeStruct(TILE, jnp.int32), f32(2 * BLK_DEV * ROWS, LANES)
        ),
        in_specs=[SMEM, VMEM, VMEM],
        out_specs=(VMEM, SMEM, VMEM),
        scratch_shapes=[
            pltpu.VMEM(TILE, jnp.int32),
            pltpu.VMEM((devs - 1,) + TILE, jnp.int32),
            pltpu.VMEM((groups - 1,) + TILE, jnp.int32),
            pltpu.VMEM(TILE, jnp.float32),
            pltpu.VMEM((devs - 1,) + TILE, jnp.float32),
            pltpu.VMEM((groups - 1,) + TILE, jnp.float32),
            pltpu.VMEM(TILE, jnp.int32),
            dma((2,)),
            dma((devs - 1,)), dma((devs - 1,)), dma((groups - 1,)), dma((groups - 1,)),
            dma((devs - 1,)), dma((devs - 1,)), dma((groups - 1,)), dma((groups - 1,)),
            dma((2,)),
        ],
        compiler_params=pltpu.CompilerParams(
            collective_id=0, has_side_effects=True, vmem_limit_bytes=LIMIT
        ),
        name="gather",
    )(counts, outgoing, rows)
    u, plo, phi = pl.pallas_call(
        assemble_kernel,
        out_shape=(f32(*SLAB), f32(*PACK), f32(*PACK)),
        in_specs=[SMEM, VMEM],
        out_specs=(VMEM,) * 3,
        compiler_params=plain,
        name="assemble",
    )(small, joined)

    def exchange(u, plo, phi, collective_id):
        return pl.pallas_call(
            functools.partial(halo_kernel, groups, devs),
            out_shape=ghosts,
            in_specs=[VMEM] * 3,
            out_specs=(VMEM,) * 4,
            scratch_shapes=[dma((4,)), dma((4,))],
            compiler_params=pltpu.CompilerParams(
                collective_id=collective_id, has_side_effects=True, vmem_limit_bytes=LIMIT
            ),
            name="halo",
        )(u, plo, phi)

    xlo, xhi, glo, ghi = exchange(u, plo, phi, 1)
    work = [
        pltpu.VMEM((BS + 4, FIELDS, YV + 2) + TILE, jnp.float32),
        pltpu.VMEM((BS + 1, FIELDS, YV) + TILE, jnp.float32),
        pltpu.VMEM((FIELDS, YV + 1) + TILE, jnp.float32),
    ]
    one, plo, phi = pl.pallas_call(
        first_kernel,
        out_shape=(f32(*SLAB), f32(*PACK), f32(*PACK)),
        in_specs=[VMEM] * 6,
        out_specs=(VMEM,) * 3,
        scratch_shapes=work,
        compiler_params=plain,
        name="first_stage",
    )(step, u, xlo, xhi, glo, ghi)

    xlo, xhi, glo, ghi = exchange(one, plo, phi, 2)
    out = pl.pallas_call(
        second_kernel,
        out_shape=f32(BLK_DEV * ROWS, LANES),
        in_specs=[VMEM] * 7,
        out_specs=VMEM,
        scratch_shapes=work,
        compiler_params=plain,
        name="second_stage",
    )(step, u, one, xlo, xhi, glo, ghi)
    out = out.reshape(BLK_DEV, CHUNKS, FIELDS, LANES).transpose(0, 2, 1, 3)
    return out.reshape(BLK_DEV, FIELDS, CHUNKS * LANES)


def solution(mesh):
    groups, devs = mesh.shape["group"], mesh.shape["dev"]
    in_specs = (P(("group", "dev"), None, None), P(("group", "dev")))
    out_specs = P(("group", "dev"), None, None)
    return jax.shard_map(
        functools.partial(body, groups, devs),
        mesh=mesh, in_specs=in_specs, out_specs=out_specs, check_vma=False,
    )
```

```python
import functools

import jax
import jax.numpy as jnp
from jax import lax
from jax.experimental import pallas as pl
from jax.experimental.pallas import tpu as pltpu
from jax.sharding import PartitionSpec as P

BS = 16
BRICK_Y = 2
BRICK_Z = 8
BLK_DEV = 16
FIELDS = 8
LANES = 128
CHUNKS = 32
ROWS = CHUNKS * FIELDS
YV = 4

GAMMA = 5.0 / 3.0
COURANT = 0.25
DENSITY_FLOOR = 0.05
PRESSURE_FLOOR = 0.05
TINY = 1.2e-38

MESH = pl.DeviceIdType.MESH


def reciprocal(x):
    guess = pl.reciprocal(x, approx=True)
    return guess * (2.0 - x * guess)


def primitive(u):
    density = jnp.maximum(u[0], DENSITY_FLOOR)
    inverse = reciprocal(density)
    vx, vy, vz = u[1] * inverse, u[2] * inverse, u[3] * inverse
    kinetic = 0.5 * density * (vx * vx + vy * vy + vz * vz)
    energy_b = 0.5 * (u[5] * u[5] + u[6] * u[6] + u[7] * u[7])
    pressure = jnp.maximum((GAMMA - 1.0) * (u[4] - kinetic - energy_b), PRESSURE_FLOOR)
    return [density, vx, vy, vz, pressure, u[5], u[6], u[7]], inverse


def fast_from(sound, alfven, along):
    total = sound + alfven
    inner = jnp.maximum(total * total - 4.0 * sound * along, TINY)
    outer = 0.5 * (total + inner * lax.rsqrt(inner))
    return outer * lax.rsqrt(outer)


def wave(w, n):
    inverse = reciprocal(w[0])
    b2 = w[5] * w[5] + w[6] * w[6] + w[7] * w[7]
    bn = w[5 + n]
    return fast_from(GAMMA * w[4] * inverse, b2 * inverse, bn * bn * inverse), 0.5 * b2


def weighted(w, half_b2, n, weight, shift):
    r, v, p, b = w[0], w[1:4], w[4], w[5:8]
    vn, bn = v[n], b[n]
    k = weight * vn + shift
    q = r * k
    wb = weight * bn
    wp = weight * (p + half_b2)
    energy = p * (1.0 / (GAMMA - 1.0)) + half_b2 + 0.5 * r * (v[0] * v[0] + v[1] * v[1] + v[2] * v[2])
    vb = v[0] * b[0] + v[1] * b[1] + v[2] * b[2]
    momentum = [v[i] * q - b[i] * wb for i in range(3)]
    momentum[n] = momentum[n] + wp
    field = [shift * bn if i == n else b[i] * k - v[i] * wb for i in range(3)]
    return [q] + momentum + [energy * k + wp * vn - wb * vb] + field


def hlle(left, right, n):
    cl, hl = wave(left, n)
    cr, hr = wave(right, n)
    vl, vr = left[1 + n], right[1 + n]
    upper = jnp.maximum(jnp.maximum(vr + cr, vl + cl), 0.0)
    lower = jnp.minimum(jnp.minimum(vl - cl, vr - cr), 0.0)
    inverse = reciprocal(upper - lower)
    a = upper * inverse
    c = a * lower
    first = weighted(left, hl, n, a, -c)
    second = weighted(right, hr, n, -lower * inverse, c)
    return [x + y for x, y in zip(first, second)]


def half_minmod(a, b):
    return 0.5 * (jnp.maximum(jnp.minimum(a, b), 0.0) + jnp.minimum(jnp.maximum(a, b), 0.0))


def roll(x, shift, axis):
    size = x.shape[axis]
    shift = shift % size
    return x if shift == 0 else pltpu.roll(x, shift, axis)


def lane_index():
    return lax.broadcasted_iota(jnp.int32, (8, LANES), 1)


def lane_gather(x, index):
    return jnp.take_along_axis(x, index, axis=1, mode="promise_in_bounds")


def z_up(tiles):
    lane = lane_index()
    edge = lane % BS == 0
    index = lane - lane % BS + (lane + 1) % BS
    moved = [jnp.where(edge, roll(x, -1, 0), x) for x in tiles]
    return jnp.stack([lane_gather(x, index) for x in moved])


def z_down(tiles):
    lane = lane_index()
    edge = lane % BS == BS - 1
    index = lane - lane % BS + (lane + BS - 1) % BS
    moved = [jnp.where(edge, roll(x, 1, 0), x) for x in tiles]
    return jnp.stack([lane_gather(x, index) for x in moved])


def split(x):
    return [x[i] for i in range(x.shape[0])]


def fill_primitives(u_ref, xlo_ref, xhi_ref, glo_ref, ghi_ref, w_ref):
    def planes(source, base):
        def one(c, carry):
            w, _ = primitive([source[c, f] for f in range(FIELDS)])
            for f in range(FIELDS):
                w_ref[base + c, f, 1:YV + 1] = w[f]
            return carry

        lax.fori_loop(0, source.shape[0], one, 0)

    planes(xlo_ref, 0)
    planes(u_ref, 2)
    planes(xhi_ref, 2 + BS)

    def ghosts(c, carry):
        for ghost, v, base in ((glo_ref, 0, 96), (ghi_ref, YV + 1, 0)):
            u = [roll(ghost[c, f // 4], base - 32 * (f % 4), 1) for f in range(FIELDS)]
            w, _ = primitive(u)
            for f in range(FIELDS):
                w_ref[c + 2, f, v] = w[f]
        return carry

    lax.fori_loop(0, BS, ghosts, 0)


PAIRS = ((0, 2), (2, 2))


def x_faces(w_ref, sx_ref, fx_ref):
    def slopes(c, carry):
        for f in range(FIELDS):
            here = w_ref[c + 1, f, 1:YV + 1]
            sx_ref[c, f] = half_minmod(
                here - w_ref[c, f, 1:YV + 1], w_ref[c + 2, f, 1:YV + 1] - here
            )
        return carry

    lax.fori_loop(0, BS + 2, slopes, 0)

    def one(face, carry):
        for v, n in PAIRS:
            left = [w_ref[face + 1, f, v + 1:v + 1 + n] + sx_ref[face, f, v:v + n] for f in range(FIELDS)]
            right = [
                w_ref[face + 2, f, v + 1:v + 1 + n] - sx_ref[face + 1, f, v:v + n]
                for f in range(FIELDS)
            ]
            for f, flux in enumerate(hlle(left, right, 0)):
                fx_ref[face, f, v:v + n] = flux
        return carry

    lax.fori_loop(0, BS + 1, one, 0)


def faces(l_ref, r_ref, f_ref, n, parts):
    for v, size in parts:
        left = [l_ref[f, v:v + size] for f in range(FIELDS)]
        right = [r_ref[f, v:v + size] for f in range(FIELDS)]
        for f, flux in enumerate(hlle(left, right, n)):
            f_ref[f, v:v + size] = flux


def y_faces(w_ref, c, l_ref, r_ref, f_ref):
    lane = lax.broadcasted_iota(jnp.int32, (YV + 2, 8, LANES), 2)
    top = lane >= LANES - BS
    bottom = lane < BS
    for f in range(FIELDS):
        w = w_ref[c + 2, f]
        rolled = roll(w, -BS, 2)
        diff = jnp.where(top, jnp.concatenate([rolled[1:], rolled[-1:]]), rolled) - w
        rolled = roll(diff, BS, 2)
        down = jnp.where(bottom, jnp.concatenate([rolled[:1], rolled[:-1]]), rolled)
        slope = half_minmod(down, diff)
        low = roll(w - slope, -BS, 2)
        l_ref[f] = (w + slope)[:YV + 1]
        r_ref[f] = jnp.where(top[1:], low[1:], low[:-1])
    faces(l_ref, r_ref, f_ref, 1, PAIRS + ((YV, 1),))


def z_faces(w_ref, c, l_ref, r_ref, f_ref):
    for f in range(FIELDS):
        w = w_ref[c + 2, f, 1:YV + 1]
        diff = z_up(split(w)) - w
        slope = half_minmod(z_down(split(diff)), diff)
        l_ref[f, 0:YV] = w + slope
        r_ref[f, 0:YV] = z_up(split(w - slope))
    faces(l_ref, r_ref, f_ref, 2, PAIRS)


def plane_change(w_ref, fx_ref, c, work):
    ly, ry, fy, lz, rz, fz = work
    y_faces(w_ref, c, ly, ry, fy)
    z_faces(w_ref, c, lz, rz, fz)
    bottom = lax.broadcasted_iota(jnp.int32, (YV, 8, LANES), 2) < BS
    out = []
    for f in range(FIELDS):
        flux = fz[f]
        across_z = flux - z_down(split(flux))
        flux = fy[f]
        rolled = roll(flux, BS, 2)
        across_y = flux[1:] - jnp.where(bottom, rolled[:-1], rolled[1:])
        out.append((fx_ref[c + 1, f] - fx_ref[c, f]) + across_y + across_z)
    return out


def pack(tiles, base):
    group = lane_index() // 32
    out = []
    for q in range(2):
        total = roll(tiles[4 * q], -base, 1)
        for k in range(1, 4):
            total = jnp.where(group == k, roll(tiles[4 * q + k], 32 * k - base, 1), total)
        out.append(total)
    return out


def first_kernel(
    step_ref, u_ref, xlo, xhi, glo, ghi, out_ref, plo_ref, phi_ref, w_ref, sx_ref, fx_ref, *work
):
    fill_primitives(u_ref, xlo, xhi, glo, ghi, w_ref)
    x_faces(w_ref, sx_ref, fx_ref)

    def one(c, carry):
        step = step_ref[...]
        change = plane_change(w_ref, fx_ref, c, work)
        low, high = [], []
        for f in range(FIELDS):
            new = u_ref[c, f] - step * change[f]
            out_ref[c, f] = new
            low.append(new[0])
            high.append(new[YV - 1])
        for q, tile in enumerate(pack(low, 0)):
            plo_ref[c, q] = tile
        for q, tile in enumerate(pack(high, 96)):
            phi_ref[c, q] = tile
        return carry

    lax.fori_loop(0, BS, one, 0)


def second_kernel(
    step_ref, u_ref, one_ref, xlo, xhi, glo, ghi, out_ref, w_ref, sx_ref, fx_ref, *work
):
    fill_primitives(one_ref, xlo, xhi, glo, ghi, w_ref)
    x_faces(w_ref, sx_ref, fx_ref)

    def one(c, carry):
        step = step_ref[...]
        change = plane_change(w_ref, fx_ref, c, work)
        for f in range(FIELDS):
            new = 0.5 * (u_ref[c, f] + one_ref[c, f] - step * change[f])
            for v in range(YV):
                row = (v // 2) * (BRICK_Z * ROWS) + (c * 2 + v % 2) * FIELDS + f
                out_ref[pl.ds(row, BRICK_Z, stride=ROWS), :] = new[v]
        return carry

    lax.fori_loop(0, BS, one, 0)


def ring(groups, devs):
    g, j = lax.axis_index("group"), lax.axis_index("dev")
    me = g * devs + j
    count = groups * devs
    after, before = lax.rem(me + 1, count), lax.rem(me + count - 1, count)
    curve_next = (after // devs, lax.rem(after, devs))
    curve_prev = (before // devs, lax.rem(before, devs))
    row = [(g, lax.rem(j + d, devs)) for d in range(1, devs)]
    column = [(lax.rem(g + d, groups), j) for d in range(1, groups)]
    return g, j, me, curve_next, curve_prev, row, column


def greet(peers):
    barrier = pltpu.get_barrier_semaphore()
    for peer in peers:
        pl.semaphore_signal(barrier, inc=1, device_id=peer, device_id_type=MESH)
    pl.semaphore_wait(barrier, len(peers))


def remote(source, target, send, recv, device):
    return pltpu.make_async_remote_copy(
        src_ref=source, dst_ref=target, send_sem=send, recv_sem=recv,
        device_id=device, device_id_type=MESH,
    )


def spread(*messages):
    copies = [
        remote(source, slots.at[d], send.at[d], recv.at[d], p)
        for source, slots, send, recv, peers in messages
        for d, p in enumerate(peers)
    ]
    for copy in copies:
        copy.start()
    for copy in copies:
        copy.wait()


def halo(g, j, groups, devs, u_ref, plo_ref, phi_ref, xlo, xhi, glo, ghi, send, recv):
    up = (lax.rem(g + 1, groups), j)
    down = (lax.rem(g + groups - 1, groups), j)
    right = (g, lax.rem(j + 1, devs))
    left = (g, lax.rem(j + devs - 1, devs))
    copies = [
        remote(u_ref.at[pl.ds(BS - 2, 2)], xlo, send.at[0], recv.at[0], up),
        remote(u_ref.at[pl.ds(0, 2)], xhi, send.at[1], recv.at[1], down),
        remote(phi_ref, glo, send.at[2], recv.at[2], right),
        remote(plo_ref, ghi, send.at[3], recv.at[3], left),
    ]
    for copy in copies:
        copy.start()
    for copy in copies:
        copy.wait()


def halo_kernel(groups, devs, u_ref, plo_ref, phi_ref, xlo, xhi, glo, ghi, send, recv):
    g, j = lax.axis_index("group"), lax.axis_index("dev")
    greet([
        (lax.rem(g + 1, groups), j),
        (lax.rem(g + groups - 1, groups), j),
        (g, lax.rem(j + 1, devs)),
        (g, lax.rem(j + devs - 1, devs)),
    ])
    halo(g, j, groups, devs, u_ref, plo_ref, phi_ref, xlo, xhi, glo, ghi, send, recv)


def signal_speed(u):
    w, inverse = primitive(u)
    b2 = [w[5 + i] * w[5 + i] for i in range(3)]
    sound = GAMMA * w[4] * inverse
    alfven = (b2[0] + b2[1] + b2[2]) * inverse
    speeds = [jnp.abs(w[1 + i]) + fast_from(sound, alfven, b2[i] * inverse) for i in range(3)]
    return jnp.maximum(jnp.maximum(speeds[0], speeds[1]), speeds[2])


def stage_kernel(count_ref, own_ref, out_ref, sem):
    copies = []
    for m in range(BLK_DEV - 1):
        base = jnp.maximum(count_ref[0] - BLK_DEV + 1 + m, 0) * ROWS
        copies.append(pltpu.make_async_copy(
            own_ref.at[pl.ds(pl.multiple_of(base, ROWS), ROWS)],
            out_ref.at[pl.ds(m * ROWS, ROWS)],
            sem.at[m],
        ))
    for copy in copies:
        copy.start()
    for copy in copies:
        copy.wait()


def gather_kernel(
    groups, devs, cap, count_ref, outgoing, own_ref,
    step_ref, small_ref, joined,
    count_msg, count_row, count_col, speed_msg, speed_row, speed_col,
    total_ref, held, block_sem, row_send, row_recv, col_send, col_recv,
    srow_send, srow_recv, scol_send, scol_recv, local_sem,
):
    g, j, me, curve_next, curve_prev, row, column = ring(groups, devs)
    staged = pltpu.make_async_copy(own_ref, held, local_sem.at[2])
    staged.start()
    greet(row + column + [curve_next, curve_prev])
    count = count_ref[0]
    blocks = remote(
        outgoing, joined.at[pl.ds(ROWS, (BLK_DEV - 1) * ROWS)], block_sem.at[0], block_sem.at[1],
        curve_next,
    )
    blocks.start()
    local = pltpu.make_async_copy(
        own_ref.at[pl.ds(0, BLK_DEV * ROWS)], joined.at[pl.ds(BLK_DEV * ROWS, BLK_DEV * ROWS)],
        local_sem.at[0],
    )
    local.start()
    staged.wait()

    slot = lax.broadcasted_iota(jnp.int32, (8, LANES), 0)

    def chunk(t, top):
        for first in list(range(0, cap - 8, 8)) + [cap - 8]:
            u = [
                held[pl.ds(first * ROWS + t * FIELDS + f, 8, stride=ROWS), :]
                for f in range(FIELDS)
            ]
            top = jnp.maximum(top, jnp.where(slot + first < count, signal_speed(u), 0.0))
        return top

    top = lax.fori_loop(0, CHUNKS, chunk, jnp.zeros((8, LANES), jnp.float32))

    count_msg[...] = jnp.full((8, LANES), count, jnp.int32)
    speed_msg[...] = top
    spread(
        (count_msg, count_row, row_send, row_recv, row),
        (speed_msg, speed_row, srow_send, srow_recv, row),
    )
    before = jnp.zeros((8, LANES), jnp.int32)
    every = count_msg[...]
    for d in range(1, devs):
        value = count_row[d - 1]
        every = every + value
        before = before + jnp.where(d <= j, value, 0)
        top = jnp.maximum(top, speed_row[d - 1])
    count_msg[...] = every
    speed_msg[...] = top
    spread(
        (count_msg, count_col, col_send, col_recv, column),
        (speed_msg, speed_col, scol_send, scol_recv, column),
    )
    for d in range(1, groups):
        before = before + jnp.where(d <= g, count_col[d - 1], 0)
        top = jnp.maximum(top, speed_col[d - 1])
    total_ref[...] = before - me * BLK_DEV
    narrow = pltpu.make_async_copy(total_ref, small_ref, local_sem.at[1])
    narrow.start()
    top = jnp.max(jnp.max(top, axis=1, keepdims=True), axis=0, keepdims=True)
    step_ref[...] = COURANT / jnp.broadcast_to(top, (8, LANES))

    narrow.wait()
    local.wait()
    blocks.wait()


def assemble_kernel(small_ref, joined, u_ref, plo, phi):
    surplus = small_ref[0, 0]

    def assemble(c, carry):
        for v in range(YV):
            for f in range(FIELDS):
                base = (BLK_DEV - surplus + (v // 2) * BRICK_Z) * ROWS
                u_ref[c, f, v] = joined[
                    pl.ds(base + (c * 2 + v % 2) * FIELDS + f, BRICK_Z, stride=ROWS), :
                ]
        for q, tile in enumerate(pack([u_ref[c, f, 0] for f in range(FIELDS)], 0)):
            plo[c, q] = tile
        for q, tile in enumerate(pack([u_ref[c, f, YV - 1] for f in range(FIELDS)], 96)):
            phi[c, q] = tile
        return carry

    lax.fori_loop(0, BS, assemble, 0)


TILE = (8, LANES)
SLAB = (BS, FIELDS, YV) + TILE
EDGE = (2, FIELDS, YV) + TILE
PACK = (BS, 2) + TILE
LIMIT = 48 * 1024 * 1024


def f32(*shape):
    return jax.ShapeDtypeStruct(shape, jnp.float32)


VMEM = pl.BlockSpec(memory_space=pltpu.VMEM)
ANY = pl.BlockSpec(memory_space=pl.ANY)
SMEM = pl.BlockSpec(memory_space=pltpu.SMEM)


def body(groups, devs, blocks_in, counts):
    cap = blocks_in.shape[0]
    rows = blocks_in.reshape(cap, FIELDS, CHUNKS, LANES).transpose(0, 2, 1, 3)
    rows = rows.reshape(cap * ROWS, LANES)
    ghosts = (f32(*EDGE), f32(*EDGE), f32(*PACK), f32(*PACK))
    dma = pltpu.SemaphoreType.DMA
    plain = pltpu.CompilerParams(vmem_limit_bytes=LIMIT)
    outgoing = pl.pallas_call(
        stage_kernel,
        out_shape=f32((BLK_DEV - 1) * ROWS, LANES),
        in_specs=[SMEM, ANY],
        out_specs=VMEM,
        scratch_shapes=[dma((BLK_DEV - 1,))],
        compiler_params=plain,
        name="stage",
    )(counts, rows)
    step, small, joined = pl.pallas_call(
        functools.partial(gather_kernel, groups, devs, cap),
        out_shape=(
            f32(*TILE), jax.ShapeDtypeStruct(TILE, jnp.int32), f32(2 * BLK_DEV * ROWS, LANES)
        ),
        in_specs=[SMEM, VMEM, ANY],
        out_specs=(VMEM, SMEM, VMEM),
        scratch_shapes=[
            pltpu.VMEM(TILE, jnp.int32),
            pltpu.VMEM((devs - 1,) + TILE, jnp.int32),
            pltpu.VMEM((groups - 1,) + TILE, jnp.int32),
            pltpu.VMEM(TILE, jnp.float32),
            pltpu.VMEM((devs - 1,) + TILE, jnp.float32),
            pltpu.VMEM((groups - 1,) + TILE, jnp.float32),
            pltpu.VMEM(TILE, jnp.int32),
            pltpu.VMEM((cap * ROWS, LANES), jnp.float32),
            dma((2,)),
            dma((devs - 1,)), dma((devs - 1,)), dma((groups - 1,)), dma((groups - 1,)),
            dma((devs - 1,)), dma((devs - 1,)), dma((groups - 1,)), dma((groups - 1,)),
            dma((3,)),
        ],
        compiler_params=pltpu.CompilerParams(
            collective_id=0, has_side_effects=True, vmem_limit_bytes=LIMIT
        ),
        name="gather",
    )(counts, outgoing, rows)
    u, plo, phi = pl.pallas_call(
        assemble_kernel,
        out_shape=(f32(*SLAB), f32(*PACK), f32(*PACK)),
        in_specs=[SMEM, VMEM],
        out_specs=(VMEM,) * 3,
        compiler_params=plain,
        name="assemble",
    )(small, joined)

    def exchange(u, plo, phi, collective_id):
        return pl.pallas_call(
            functools.partial(halo_kernel, groups, devs),
            out_shape=ghosts,
            in_specs=[VMEM] * 3,
            out_specs=(VMEM,) * 4,
            scratch_shapes=[dma((4,)), dma((4,))],
            compiler_params=pltpu.CompilerParams(
                collective_id=collective_id, has_side_effects=True, vmem_limit_bytes=LIMIT
            ),
            name="halo",
        )(u, plo, phi)

    xlo, xhi, glo, ghi = exchange(u, plo, phi, 1)
    work = [
        pltpu.VMEM((BS + 4, FIELDS, YV + 2) + TILE, jnp.float32),
        pltpu.VMEM((BS + 2, FIELDS, YV) + TILE, jnp.float32),
        pltpu.VMEM((BS + 1, FIELDS, YV) + TILE, jnp.float32),
    ] + [pltpu.VMEM((FIELDS, YV + 1) + TILE, jnp.float32)] * 3 + [
        pltpu.VMEM((FIELDS, YV) + TILE, jnp.float32)
    ] * 3
    one, plo, phi = pl.pallas_call(
        first_kernel,
        out_shape=(f32(*SLAB), f32(*PACK), f32(*PACK)),
        in_specs=[VMEM] * 6,
        out_specs=(VMEM,) * 3,
        scratch_shapes=work,
        compiler_params=plain,
        name="first_stage",
    )(step, u, xlo, xhi, glo, ghi)

    xlo, xhi, glo, ghi = exchange(one, plo, phi, 2)
    out = pl.pallas_call(
        second_kernel,
        out_shape=f32(BLK_DEV * ROWS, LANES),
        in_specs=[VMEM] * 7,
        out_specs=VMEM,
        scratch_shapes=work,
        compiler_params=plain,
        name="second_stage",
    )(step, u, one, xlo, xhi, glo, ghi)
    out = out.reshape(BLK_DEV, CHUNKS, FIELDS, LANES).transpose(0, 2, 1, 3)
    return out.reshape(BLK_DEV, FIELDS, CHUNKS * LANES)


def solution(mesh):
    groups, devs = mesh.shape["group"], mesh.shape["dev"]
    in_specs = (P(("group", "dev"), None, None), P(("group", "dev")))
    out_specs = P(("group", "dev"), None, None)
    return jax.shard_map(
        functools.partial(body, groups, devs),
        mesh=mesh, in_specs=in_specs, out_specs=out_specs, check_vma=False,
    )
```

```python
import functools

import jax
import jax.numpy as jnp
from jax import lax
from jax.experimental import pallas as pl
from jax.experimental.pallas import tpu as pltpu
from jax.sharding import PartitionSpec as P

BS = 16
BRICK_Y = 2
BRICK_Z = 8
BLK_DEV = 16
FIELDS = 8
LANES = 128
CHUNKS = 32
ROWS = CHUNKS * FIELDS
YV = 4

GAMMA = 5.0 / 3.0
COURANT = 0.25
DENSITY_FLOOR = 0.05
PRESSURE_FLOOR = 0.05
TINY = 1.2e-38

MESH = pl.DeviceIdType.MESH


def reciprocal(x):
    guess = pl.reciprocal(x, approx=True)
    return guess * (2.0 - x * guess)


def primitive(u):
    density = jnp.maximum(u[0], DENSITY_FLOOR)
    inverse = reciprocal(density)
    vx, vy, vz = u[1] * inverse, u[2] * inverse, u[3] * inverse
    kinetic = 0.5 * density * (vx * vx + vy * vy + vz * vz)
    energy_b = 0.5 * (u[5] * u[5] + u[6] * u[6] + u[7] * u[7])
    pressure = jnp.maximum((GAMMA - 1.0) * (u[4] - kinetic - energy_b), PRESSURE_FLOOR)
    return [density, vx, vy, vz, pressure, u[5], u[6], u[7]], inverse


def fast_from(sound, alfven, along):
    total = sound + alfven
    inner = jnp.maximum(total * total - 4.0 * sound * along, TINY)
    outer = 0.5 * (total + inner * lax.rsqrt(inner))
    return outer * lax.rsqrt(outer)


def wave(w, n):
    inverse = reciprocal(w[0])
    b2 = w[5] * w[5] + w[6] * w[6] + w[7] * w[7]
    bn = w[5 + n]
    return fast_from(GAMMA * w[4] * inverse, b2 * inverse, bn * bn * inverse), 0.5 * b2


def weighted(w, half_b2, n, weight, shift):
    r, v, p, b = w[0], w[1:4], w[4], w[5:8]
    vn, bn = v[n], b[n]
    k = weight * vn + shift
    q = r * k
    wb = weight * bn
    wp = weight * (p + half_b2)
    energy = p * (1.0 / (GAMMA - 1.0)) + half_b2 + 0.5 * r * (v[0] * v[0] + v[1] * v[1] + v[2] * v[2])
    vb = v[0] * b[0] + v[1] * b[1] + v[2] * b[2]
    momentum = [v[i] * q - b[i] * wb for i in range(3)]
    momentum[n] = momentum[n] + wp
    field = [shift * bn if i == n else b[i] * k - v[i] * wb for i in range(3)]
    return [q] + momentum + [energy * k + wp * vn - wb * vb] + field


def hlle(left, right, n):
    cl, hl = wave(left, n)
    cr, hr = wave(right, n)
    vl, vr = left[1 + n], right[1 + n]
    upper = jnp.maximum(jnp.maximum(vr + cr, vl + cl), 0.0)
    lower = jnp.minimum(jnp.minimum(vl - cl, vr - cr), 0.0)
    inverse = reciprocal(upper - lower)
    a = upper * inverse
    c = a * lower
    first = weighted(left, hl, n, a, -c)
    second = weighted(right, hr, n, -lower * inverse, c)
    return [x + y for x, y in zip(first, second)]


def half_minmod(a, b):
    return 0.5 * (jnp.maximum(jnp.minimum(a, b), 0.0) + jnp.minimum(jnp.maximum(a, b), 0.0))


def roll(x, shift, axis):
    size = x.shape[axis]
    shift = shift % size
    return x if shift == 0 else pltpu.roll(x, shift, axis)


def lane_index():
    return lax.broadcasted_iota(jnp.int32, (8, LANES), 1)


def lane_gather(x, index):
    return jnp.take_along_axis(x, index, axis=1, mode="promise_in_bounds")


def z_up(tiles):
    lane = lane_index()
    edge = lane % BS == 0
    index = lane - lane % BS + (lane + 1) % BS
    moved = [jnp.where(edge, roll(x, -1, 0), x) for x in tiles]
    return jnp.stack([lane_gather(x, index) for x in moved])


def z_down(tiles):
    lane = lane_index()
    edge = lane % BS == BS - 1
    index = lane - lane % BS + (lane + BS - 1) % BS
    moved = [jnp.where(edge, roll(x, 1, 0), x) for x in tiles]
    return jnp.stack([lane_gather(x, index) for x in moved])


def split(x):
    return [x[i] for i in range(x.shape[0])]


def fill_planes(source, w_ref, base):
    def one(c, carry):
        w, _ = primitive([source[c, f] for f in range(FIELDS)])
        for f in range(FIELDS):
            w_ref[base + c, f, 1:YV + 1] = w[f]
        return carry

    lax.fori_loop(0, source.shape[0], one, 0)


def fill_ghosts(glo_ref, ghi_ref, w_ref):
    def one(c, carry):
        for ghost, v, base in ((glo_ref, 0, 96), (ghi_ref, YV + 1, 0)):
            u = [roll(ghost[c, f // 4], base - 32 * (f % 4), 1) for f in range(FIELDS)]
            w, _ = primitive(u)
            for f in range(FIELDS):
                w_ref[c + 2, f, v] = w[f]
        return carry

    lax.fori_loop(0, BS, one, 0)


PAIRS = ((0, 2), (2, 2))


def x_faces(w_ref, sx_ref, fx_ref):
    def slopes(c, carry):
        for f in range(FIELDS):
            here = w_ref[c + 1, f, 1:YV + 1]
            sx_ref[c, f] = half_minmod(
                here - w_ref[c, f, 1:YV + 1], w_ref[c + 2, f, 1:YV + 1] - here
            )
        return carry

    lax.fori_loop(0, BS + 2, slopes, 0)

    def one(face, carry):
        for v, n in PAIRS:
            left = [w_ref[face + 1, f, v + 1:v + 1 + n] + sx_ref[face, f, v:v + n] for f in range(FIELDS)]
            right = [
                w_ref[face + 2, f, v + 1:v + 1 + n] - sx_ref[face + 1, f, v:v + n]
                for f in range(FIELDS)
            ]
            for f, flux in enumerate(hlle(left, right, 0)):
                fx_ref[face, f, v:v + n] = flux
        return carry

    lax.fori_loop(0, BS + 1, one, 0)


def faces(l_ref, r_ref, f_ref, n, parts):
    for v, size in parts:
        left = [l_ref[f, v:v + size] for f in range(FIELDS)]
        right = [r_ref[f, v:v + size] for f in range(FIELDS)]
        for f, flux in enumerate(hlle(left, right, n)):
            f_ref[f, v:v + size] = flux


def y_faces(w_ref, c, l_ref, r_ref, f_ref):
    lane = lax.broadcasted_iota(jnp.int32, (YV + 2, 8, LANES), 2)
    top = lane >= LANES - BS
    bottom = lane < BS
    for f in range(FIELDS):
        w = w_ref[c + 2, f]
        rolled = roll(w, -BS, 2)
        diff = jnp.where(top, jnp.concatenate([rolled[1:], rolled[-1:]]), rolled) - w
        rolled = roll(diff, BS, 2)
        down = jnp.where(bottom, jnp.concatenate([rolled[:1], rolled[:-1]]), rolled)
        slope = half_minmod(down, diff)
        low = roll(w - slope, -BS, 2)
        l_ref[f] = (w + slope)[:YV + 1]
        r_ref[f] = jnp.where(top[1:], low[1:], low[:-1])
    faces(l_ref, r_ref, f_ref, 1, PAIRS + ((YV, 1),))


def z_faces(w_ref, c, l_ref, r_ref, f_ref):
    for f in range(FIELDS):
        w = w_ref[c + 2, f, 1:YV + 1]
        diff = z_up(split(w)) - w
        slope = half_minmod(z_down(split(diff)), diff)
        l_ref[f, 0:YV] = w + slope
        r_ref[f, 0:YV] = z_up(split(w - slope))
    faces(l_ref, r_ref, f_ref, 2, PAIRS)


def z_pass(w_ref, acc_ref, lz, rz, fz):
    def one(c, carry):
        z_faces(w_ref, c, lz, rz, fz)
        for f in range(FIELDS):
            flux = fz[f]
            acc_ref[c, f] = flux - z_down(split(flux))
        return carry

    lax.fori_loop(0, BS, one, 0)


def y_pass(w_ref, acc_ref, ly, ry, fy):
    bottom = lax.broadcasted_iota(jnp.int32, (YV, 8, LANES), 2) < BS

    def one(c, carry):
        y_faces(w_ref, c, ly, ry, fy)
        for f in range(FIELDS):
            flux = fy[f]
            rolled = roll(flux, BS, 2)
            across = flux[1:] - jnp.where(bottom, rolled[:-1], rolled[1:])
            acc_ref[c, f] = across + acc_ref[c, f]
        return carry

    lax.fori_loop(0, BS, one, 0)


def pack(tiles, base):
    group = lane_index() // 32
    out = []
    for q in range(2):
        total = roll(tiles[4 * q], -base, 1)
        for k in range(1, 4):
            total = jnp.where(group == k, roll(tiles[4 * q + k], 32 * k - base, 1), total)
        out.append(total)
    return out


def ring(groups, devs):
    g, j = lax.axis_index("group"), lax.axis_index("dev")
    me = g * devs + j
    count = groups * devs
    after, before = lax.rem(me + 1, count), lax.rem(me + count - 1, count)
    curve_next = (after // devs, lax.rem(after, devs))
    curve_prev = (before // devs, lax.rem(before, devs))
    row = [(g, lax.rem(j + d, devs)) for d in range(1, devs)]
    column = [(lax.rem(g + d, groups), j) for d in range(1, groups)]
    return g, j, me, curve_next, curve_prev, row, column


def greet(peers):
    barrier = pltpu.get_barrier_semaphore()
    for peer in peers:
        pl.semaphore_signal(barrier, inc=1, device_id=peer, device_id_type=MESH)
    pl.semaphore_wait(barrier, len(peers))


def remote(source, target, send, recv, device):
    return pltpu.make_async_remote_copy(
        src_ref=source, dst_ref=target, send_sem=send, recv_sem=recv,
        device_id=device, device_id_type=MESH,
    )


def messages(source, slots, send, recv, peers):
    return [remote(source, slots.at[d], send.at[d], recv.at[d], p) for d, p in enumerate(peers)]


def begin(copies):
    for copy in copies:
        copy.start()


def finish(copies):
    for copy in copies:
        copy.wait()


def step_kernel(
    groups, devs, top_ref, u_ref, plo, phi, out_ref,
    w_ref, sx_ref, fx_ref, acc_ref, one_ref, edge_lo, edge_hi, plo2, phi2,
    xlo, xhi, glo, ghi, xlo2, xhi2, glo2, ghi2, ly, ry, fy, lz, rz, fz,
    speed_msg, speed_row, speed_col, step_ref,
    row_send, row_recv, col_send, col_recv, send, recv, send2, recv2,
):
    g, j, _, _, _, row, column = ring(groups, devs)
    greet(row + column)
    up = (lax.rem(g + 1, groups), j)
    down = (lax.rem(g + groups - 1, groups), j)
    right = (g, lax.rem(j + 1, devs))
    left = (g, lax.rem(j + devs - 1, devs))
    speeds = messages(top_ref, speed_row, row_send, row_recv, row)
    begin(speeds)
    y_copies = [
        remote(phi, glo, send.at[2], recv.at[2], right),
        remote(plo, ghi, send.at[3], recv.at[3], left),
    ]
    begin(y_copies)
    x_copies = [
        remote(u_ref.at[pl.ds(BS - 2, 2)], xlo, send.at[0], recv.at[0], up),
        remote(u_ref.at[pl.ds(0, 2)], xhi, send.at[1], recv.at[1], down),
    ]
    begin(x_copies)

    fill_planes(u_ref, w_ref, 2)
    z_pass(w_ref, acc_ref, lz, rz, fz)

    finish(speeds)
    top = top_ref[...]
    for d in range(devs - 1):
        top = jnp.maximum(top, speed_row[d])
    speed_msg[...] = top
    speeds = messages(speed_msg, speed_col, col_send, col_recv, column)
    begin(speeds)

    finish(y_copies)
    fill_ghosts(glo, ghi, w_ref)
    y_pass(w_ref, acc_ref, ly, ry, fy)
    finish(x_copies)
    fill_planes(xlo, w_ref, 0)
    fill_planes(xhi, w_ref, BS + 2)
    x_faces(w_ref, sx_ref, fx_ref)

    finish(speeds)
    top = speed_msg[...]
    for d in range(groups - 1):
        top = jnp.maximum(top, speed_col[d])
    top = jnp.max(jnp.max(top, axis=1, keepdims=True), axis=0, keepdims=True)
    step_ref[...] = COURANT / jnp.broadcast_to(top, (8, LANES))

    def update(c, edge, place):
        step = step_ref[...]
        low, high = [], []
        for f in range(FIELDS):
            change = (fx_ref[c + 1, f] - fx_ref[c, f]) + acc_ref[c, f]
            new = u_ref[c, f] - step * change
            one_ref[c, f] = new
            if edge is not None:
                edge[place, f] = new
            low.append(new[0])
            high.append(new[YV - 1])
        for q, tile in enumerate(pack(low, 0)):
            plo2[c, q] = tile
        for q, tile in enumerate(pack(high, 96)):
            phi2[c, q] = tile

    def middle(c, carry):
        update(c, None, 0)
        return carry

    for place in range(2):
        update(place, edge_lo, place)
        update(BS - 2 + place, edge_hi, place)
    x_copies = [
        remote(edge_hi, xlo2, send2.at[0], recv2.at[0], up),
        remote(edge_lo, xhi2, send2.at[1], recv2.at[1], down),
    ]
    begin(x_copies)
    lax.fori_loop(2, BS - 2, middle, 0)
    y_copies = [
        remote(phi2, glo2, send2.at[2], recv2.at[2], right),
        remote(plo2, ghi2, send2.at[3], recv2.at[3], left),
    ]
    begin(y_copies)

    fill_planes(one_ref, w_ref, 2)
    z_pass(w_ref, acc_ref, lz, rz, fz)
    finish(y_copies)
    fill_ghosts(glo2, ghi2, w_ref)
    y_pass(w_ref, acc_ref, ly, ry, fy)
    finish(x_copies)
    fill_planes(xlo2, w_ref, 0)
    fill_planes(xhi2, w_ref, BS + 2)
    x_faces(w_ref, sx_ref, fx_ref)

    def last(c, carry):
        step = step_ref[...]
        for f in range(FIELDS):
            change = (fx_ref[c + 1, f] - fx_ref[c, f]) + acc_ref[c, f]
            new = 0.5 * (u_ref[c, f] + one_ref[c, f] - step * change)
            for v in range(YV):
                row = (v // 2) * (BRICK_Z * ROWS) + (c * 2 + v % 2) * FIELDS + f
                out_ref[pl.ds(row, BRICK_Z, stride=ROWS), :] = new[v]
        return carry

    lax.fori_loop(0, BS, last, 0)


def signal_speed(u):
    w, inverse = primitive(u)
    b2 = [w[5 + i] * w[5 + i] for i in range(3)]
    sound = GAMMA * w[4] * inverse
    alfven = (b2[0] + b2[1] + b2[2]) * inverse
    speeds = [jnp.abs(w[1 + i]) + fast_from(sound, alfven, b2[i] * inverse) for i in range(3)]
    return jnp.maximum(jnp.maximum(speeds[0], speeds[1]), speeds[2])


def stage_kernel(count_ref, own_ref, out_ref, sem):
    copies = []
    for m in range(BLK_DEV - 1):
        base = jnp.maximum(count_ref[0] - BLK_DEV + 1 + m, 0) * ROWS
        copies.append(pltpu.make_async_copy(
            own_ref.at[pl.ds(pl.multiple_of(base, ROWS), ROWS)],
            out_ref.at[pl.ds(m * ROWS, ROWS)],
            sem.at[m],
        ))
    for copy in copies:
        copy.start()
    for copy in copies:
        copy.wait()


def gather_kernel(
    groups, devs, cap, count_ref, outgoing, own_ref,
    top_ref, small_ref, joined,
    count_msg, row_msg, count_row, count_col, total_ref, held,
    block_sem, row_send, row_recv, col_send, col_recv, local_sem,
):
    g, j, me, curve_next, curve_prev, row, column = ring(groups, devs)
    staged = pltpu.make_async_copy(own_ref, held, local_sem.at[2])
    staged.start()
    greet(row + column + [curve_next, curve_prev])
    count = count_ref[0]
    count_msg[...] = jnp.full((8, LANES), count, jnp.int32)
    counts = messages(count_msg, count_row, row_send, row_recv, row)
    begin(counts)
    blocks = remote(
        outgoing, joined.at[pl.ds(ROWS, (BLK_DEV - 1) * ROWS)], block_sem.at[0], block_sem.at[1],
        curve_next,
    )
    blocks.start()
    local = pltpu.make_async_copy(
        own_ref.at[pl.ds(0, BLK_DEV * ROWS)], joined.at[pl.ds(BLK_DEV * ROWS, BLK_DEV * ROWS)],
        local_sem.at[0],
    )
    local.start()

    finish(counts)
    before = jnp.zeros((8, LANES), jnp.int32)
    every = count_msg[...]
    for d in range(1, devs):
        value = count_row[d - 1]
        every = every + value
        before = before + jnp.where(d <= j, value, 0)
    row_msg[...] = every
    counts = messages(row_msg, count_col, col_send, col_recv, column)
    begin(counts)

    staged.wait()
    slot = lax.broadcasted_iota(jnp.int32, (8, LANES), 0)

    def chunk(t, top):
        for first in list(range(0, cap - 8, 8)) + [cap - 8]:
            u = [
                held[pl.ds(first * ROWS + t * FIELDS + f, 8, stride=ROWS), :]
                for f in range(FIELDS)
            ]
            top = jnp.maximum(top, jnp.where(slot + first < count, signal_speed(u), 0.0))
        return top

    top_ref[...] = lax.fori_loop(0, CHUNKS, chunk, jnp.zeros((8, LANES), jnp.float32))

    finish(counts)
    for d in range(1, groups):
        before = before + jnp.where(d <= g, count_col[d - 1], 0)
    total_ref[...] = before - me * BLK_DEV
    narrow = pltpu.make_async_copy(total_ref, small_ref, local_sem.at[1])
    narrow.start()
    narrow.wait()
    local.wait()
    blocks.wait()


def assemble_kernel(small_ref, joined, u_ref, plo, phi):
    surplus = small_ref[0, 0]

    def assemble(c, carry):
        for v in range(YV):
            for f in range(FIELDS):
                base = (BLK_DEV - surplus + (v // 2) * BRICK_Z) * ROWS
                u_ref[c, f, v] = joined[
                    pl.ds(base + (c * 2 + v % 2) * FIELDS + f, BRICK_Z, stride=ROWS), :
                ]
        for q, tile in enumerate(pack([u_ref[c, f, 0] for f in range(FIELDS)], 0)):
            plo[c, q] = tile
        for q, tile in enumerate(pack([u_ref[c, f, YV - 1] for f in range(FIELDS)], 96)):
            phi[c, q] = tile
        return carry

    lax.fori_loop(0, BS, assemble, 0)


TILE = (8, LANES)
SLAB = (BS, FIELDS, YV) + TILE
EDGE = (2, FIELDS, YV) + TILE
PACK = (BS, 2) + TILE
LIMIT = 48 * 1024 * 1024


def f32(*shape):
    return jax.ShapeDtypeStruct(shape, jnp.float32)


VMEM = pl.BlockSpec(memory_space=pltpu.VMEM)
ANY = pl.BlockSpec(memory_space=pl.ANY)
SMEM = pl.BlockSpec(memory_space=pltpu.SMEM)


def body(groups, devs, blocks_in, counts):
    cap = blocks_in.shape[0]
    rows = blocks_in.reshape(cap, FIELDS, CHUNKS, LANES).transpose(0, 2, 1, 3)
    rows = rows.reshape(cap * ROWS, LANES)
    dma = pltpu.SemaphoreType.DMA
    plain = pltpu.CompilerParams(vmem_limit_bytes=LIMIT)
    outgoing = pl.pallas_call(
        stage_kernel,
        out_shape=f32((BLK_DEV - 1) * ROWS, LANES),
        in_specs=[SMEM, ANY],
        out_specs=VMEM,
        scratch_shapes=[dma((BLK_DEV - 1,))],
        compiler_params=plain,
        name="stage",
    )(counts, rows)
    top, small, joined = pl.pallas_call(
        functools.partial(gather_kernel, groups, devs, cap),
        out_shape=(
            f32(*TILE), jax.ShapeDtypeStruct(TILE, jnp.int32), f32(2 * BLK_DEV * ROWS, LANES)
        ),
        in_specs=[SMEM, VMEM, ANY],
        out_specs=(VMEM, SMEM, VMEM),
        scratch_shapes=[
            pltpu.VMEM(TILE, jnp.int32),
            pltpu.VMEM(TILE, jnp.int32),
            pltpu.VMEM((devs - 1,) + TILE, jnp.int32),
            pltpu.VMEM((groups - 1,) + TILE, jnp.int32),
            pltpu.VMEM(TILE, jnp.int32),
            pltpu.VMEM((cap * ROWS, LANES), jnp.float32),
            dma((2,)),
            dma((devs - 1,)), dma((devs - 1,)), dma((groups - 1,)), dma((groups - 1,)),
            dma((3,)),
        ],
        compiler_params=pltpu.CompilerParams(
            collective_id=0, has_side_effects=True, vmem_limit_bytes=LIMIT
        ),
        name="gather",
    )(counts, outgoing, rows)
    u, plo, phi = pl.pallas_call(
        assemble_kernel,
        out_shape=(f32(*SLAB), f32(*PACK), f32(*PACK)),
        in_specs=[SMEM, VMEM],
        out_specs=(VMEM,) * 3,
        compiler_params=plain,
        name="assemble",
    )(small, joined)

    def vmem(*shape):
        return pltpu.VMEM(shape, jnp.float32)

    ghosts = [vmem(*EDGE), vmem(*EDGE), vmem(*PACK), vmem(*PACK)]
    out = pl.pallas_call(
        functools.partial(step_kernel, groups, devs),
        out_shape=f32(BLK_DEV * ROWS, LANES),
        in_specs=[VMEM] * 4,
        out_specs=VMEM,
        scratch_shapes=[
            vmem(BS + 4, FIELDS, YV + 2, *TILE),
            vmem(BS + 2, FIELDS, YV, *TILE),
            vmem(BS + 1, FIELDS, YV, *TILE),
            vmem(*SLAB),
            vmem(*SLAB),
        ] + ghosts + ghosts + ghosts + [vmem(FIELDS, YV + 1, *TILE)] * 3
        + [vmem(FIELDS, YV, *TILE)] * 3 + [
            vmem(*TILE), vmem(devs - 1, *TILE), vmem(groups - 1, *TILE), vmem(*TILE),
            dma((devs - 1,)), dma((devs - 1,)), dma((groups - 1,)), dma((groups - 1,)),
            dma((4,)), dma((4,)), dma((4,)), dma((4,)),
        ],
        compiler_params=pltpu.CompilerParams(
            collective_id=1, has_side_effects=True, vmem_limit_bytes=LIMIT
        ),
        name="step",
    )(top, u, plo, phi)
    out = out.reshape(BLK_DEV, CHUNKS, FIELDS, LANES).transpose(0, 2, 1, 3)
    return out.reshape(BLK_DEV, FIELDS, CHUNKS * LANES)


def solution(mesh):
    groups, devs = mesh.shape["group"], mesh.shape["dev"]
    in_specs = (P(("group", "dev"), None, None), P(("group", "dev")))
    out_specs = P(("group", "dev"), None, None)
    return jax.shard_map(
        functools.partial(body, groups, devs),
        mesh=mesh, in_specs=in_specs, out_specs=out_specs, check_vma=False,
    )
```

```python
import functools

import jax
import jax.numpy as jnp
from jax import lax
from jax.experimental import pallas as pl
from jax.experimental.pallas import tpu as pltpu
from jax.sharding import PartitionSpec as P

BS = 16
BRICK_Y = 2
BRICK_Z = 8
BLK_DEV = 16
FIELDS = 8
LANES = 128
CHUNKS = 32
ROWS = CHUNKS * FIELDS
YV = 4

GAMMA = 5.0 / 3.0
COURANT = 0.25
DENSITY_FLOOR = 0.05
PRESSURE_FLOOR = 0.05
TINY = 1.2e-38

MESH = pl.DeviceIdType.MESH


def reciprocal(x):
    guess = pl.reciprocal(x, approx=True)
    return guess * (2.0 - x * guess)


def primitive(u):
    density = jnp.maximum(u[0], DENSITY_FLOOR)
    inverse = reciprocal(density)
    vx, vy, vz = u[1] * inverse, u[2] * inverse, u[3] * inverse
    kinetic = 0.5 * density * (vx * vx + vy * vy + vz * vz)
    energy_b = 0.5 * (u[5] * u[5] + u[6] * u[6] + u[7] * u[7])
    pressure = jnp.maximum((GAMMA - 1.0) * (u[4] - kinetic - energy_b), PRESSURE_FLOOR)
    return [density, vx, vy, vz, pressure, u[5], u[6], u[7]], inverse


def fast_from(sound, alfven, along):
    total = sound + alfven
    inner = jnp.maximum(total * total - 4.0 * sound * along, TINY)
    outer = 0.5 * (total + inner * lax.rsqrt(inner))
    return outer * lax.rsqrt(outer)


def wave(w, n):
    inverse = reciprocal(w[0])
    b2 = w[5] * w[5] + w[6] * w[6] + w[7] * w[7]
    bn = w[5 + n]
    return fast_from(GAMMA * w[4] * inverse, b2 * inverse, bn * bn * inverse), 0.5 * b2


def weighted(w, half_b2, n, weight, shift):
    r, v, p, b = w[0], w[1:4], w[4], w[5:8]
    vn, bn = v[n], b[n]
    k = weight * vn + shift
    q = r * k
    wb = weight * bn
    wp = weight * (p + half_b2)
    energy = p * (1.0 / (GAMMA - 1.0)) + half_b2 + 0.5 * r * (v[0] * v[0] + v[1] * v[1] + v[2] * v[2])
    vb = v[0] * b[0] + v[1] * b[1] + v[2] * b[2]
    momentum = [v[i] * q - b[i] * wb for i in range(3)]
    momentum[n] = momentum[n] + wp
    field = [shift * bn if i == n else b[i] * k - v[i] * wb for i in range(3)]
    return [q] + momentum + [energy * k + wp * vn - wb * vb] + field


def hlle(left, right, n):
    cl, hl = wave(left, n)
    cr, hr = wave(right, n)
    vl, vr = left[1 + n], right[1 + n]
    upper = jnp.maximum(jnp.maximum(vr + cr, vl + cl), 0.0)
    lower = jnp.minimum(jnp.minimum(vl - cl, vr - cr), 0.0)
    inverse = reciprocal(upper - lower)
    a = upper * inverse
    c = a * lower
    first = weighted(left, hl, n, a, -c)
    second = weighted(right, hr, n, -lower * inverse, c)
    return [x + y for x, y in zip(first, second)]


def half_minmod(a, b):
    return 0.5 * (jnp.maximum(jnp.minimum(a, b), 0.0) + jnp.minimum(jnp.maximum(a, b), 0.0))


def roll(x, shift, axis):
    size = x.shape[axis]
    shift = shift % size
    return x if shift == 0 else pltpu.roll(x, shift, axis)


def lane_index():
    return lax.broadcasted_iota(jnp.int32, (8, LANES), 1)


def lane_gather(x, index):
    return jnp.take_along_axis(x, index, axis=1, mode="promise_in_bounds")


def z_up(tiles):
    lane = lane_index()
    edge = lane % BS == 0
    index = lane - lane % BS + (lane + 1) % BS
    moved = [jnp.where(edge, roll(x, -1, 0), x) for x in tiles]
    return jnp.stack([lane_gather(x, index) for x in moved])


def z_down(tiles):
    lane = lane_index()
    edge = lane % BS == BS - 1
    index = lane - lane % BS + (lane + BS - 1) % BS
    moved = [jnp.where(edge, roll(x, 1, 0), x) for x in tiles]
    return jnp.stack([lane_gather(x, index) for x in moved])


def split(x):
    return [x[i] for i in range(x.shape[0])]


def fill_planes(source, w_ref, base):
    def one(c, carry):
        w, _ = primitive([source[c, f] for f in range(FIELDS)])
        for f in range(FIELDS):
            w_ref[base + c, f, 1:YV + 1] = w[f]
        return carry

    lax.fori_loop(0, source.shape[0], one, 0)


def fill_ghosts(glo_ref, ghi_ref, w_ref):
    def one(c, carry):
        for ghost, v, base in ((glo_ref, 0, 96), (ghi_ref, YV + 1, 0)):
            u = [roll(ghost[c, f // 4], base - 32 * (f % 4), 1) for f in range(FIELDS)]
            w, _ = primitive(u)
            for f in range(FIELDS):
                w_ref[c + 2, f, v] = w[f]
        return carry

    lax.fori_loop(0, BS, one, 0)


PAIRS = ((0, 2), (2, 2))


def x_faces(w_ref, sx_ref, fx_ref):
    def slopes(c, carry):
        for f in range(FIELDS):
            here = w_ref[c + 1, f, 1:YV + 1]
            sx_ref[c, f] = half_minmod(
                here - w_ref[c, f, 1:YV + 1], w_ref[c + 2, f, 1:YV + 1] - here
            )
        return carry

    lax.fori_loop(0, BS + 2, slopes, 0)

    def one(face, carry):
        for v, n in PAIRS:
            left = [w_ref[face + 1, f, v + 1:v + 1 + n] + sx_ref[face, f, v:v + n] for f in range(FIELDS)]
            right = [
                w_ref[face + 2, f, v + 1:v + 1 + n] - sx_ref[face + 1, f, v:v + n]
                for f in range(FIELDS)
            ]
            for f, flux in enumerate(hlle(left, right, 0)):
                fx_ref[face, f, v:v + n] = flux
        return carry

    lax.fori_loop(0, BS + 1, one, 0)


def faces(l_ref, r_ref, f_ref, n, parts):
    for v, size in parts:
        left = [l_ref[f, v:v + size] for f in range(FIELDS)]
        right = [r_ref[f, v:v + size] for f in range(FIELDS)]
        for f, flux in enumerate(hlle(left, right, n)):
            f_ref[f, v:v + size] = flux


def y_faces(w_ref, c, l_ref, r_ref, f_ref):
    lane = lax.broadcasted_iota(jnp.int32, (YV + 2, 8, LANES), 2)
    top = lane >= LANES - BS
    bottom = lane < BS
    for f in range(FIELDS):
        w = w_ref[c + 2, f]
        rolled = roll(w, -BS, 2)
        diff = jnp.where(top, jnp.concatenate([rolled[1:], rolled[-1:]]), rolled) - w
        rolled = roll(diff, BS, 2)
        down = jnp.where(bottom, jnp.concatenate([rolled[:1], rolled[:-1]]), rolled)
        slope = half_minmod(down, diff)
        low = roll(w - slope, -BS, 2)
        l_ref[f] = (w + slope)[:YV + 1]
        r_ref[f] = jnp.where(top[1:], low[1:], low[:-1])
    faces(l_ref, r_ref, f_ref, 1, PAIRS + ((YV, 1),))


def z_faces(w_ref, c, l_ref, r_ref, f_ref):
    for f in range(FIELDS):
        w = w_ref[c + 2, f, 1:YV + 1]
        diff = z_up(split(w)) - w
        slope = half_minmod(z_down(split(diff)), diff)
        l_ref[f, 0:YV] = w + slope
        r_ref[f, 0:YV] = z_up(split(w - slope))
    faces(l_ref, r_ref, f_ref, 2, PAIRS)


def z_pass(w_ref, acc_ref, lz, rz, fz):
    def one(c, carry):
        z_faces(w_ref, c, lz, rz, fz)
        for f in range(FIELDS):
            flux = fz[f]
            acc_ref[c, f] = flux - z_down(split(flux))
        return carry

    lax.fori_loop(0, BS, one, 0)


def y_pass(w_ref, acc_ref, ly, ry, fy):
    bottom = lax.broadcasted_iota(jnp.int32, (YV, 8, LANES), 2) < BS

    def one(c, carry):
        y_faces(w_ref, c, ly, ry, fy)
        for f in range(FIELDS):
            flux = fy[f]
            rolled = roll(flux, BS, 2)
            across = flux[1:] - jnp.where(bottom, rolled[:-1], rolled[1:])
            acc_ref[c, f] = across + acc_ref[c, f]
        return carry

    lax.fori_loop(0, BS, one, 0)


def pack(tiles, base):
    group = lane_index() // 32
    out = []
    for q in range(2):
        total = roll(tiles[4 * q], -base, 1)
        for k in range(1, 4):
            total = jnp.where(group == k, roll(tiles[4 * q + k], 32 * k - base, 1), total)
        out.append(total)
    return out


def ring(groups, devs):
    g, j = lax.axis_index("group"), lax.axis_index("dev")
    me = g * devs + j
    count = groups * devs
    after, before = lax.rem(me + 1, count), lax.rem(me + count - 1, count)
    curve_next = (after // devs, lax.rem(after, devs))
    curve_prev = (before // devs, lax.rem(before, devs))
    row = [(g, lax.rem(j + d, devs)) for d in range(1, devs)]
    column = [(lax.rem(g + d, groups), j) for d in range(1, groups)]
    return g, j, me, curve_next, curve_prev, row, column


def greet(peers):
    barrier = pltpu.get_barrier_semaphore()
    for peer in peers:
        pl.semaphore_signal(barrier, inc=1, device_id=peer, device_id_type=MESH)
    pl.semaphore_wait(barrier, len(peers))


def remote(source, target, send, recv, device):
    return pltpu.make_async_remote_copy(
        src_ref=source, dst_ref=target, send_sem=send, recv_sem=recv,
        device_id=device, device_id_type=MESH,
    )


def messages(source, slots, send, recv, peers):
    return [remote(source, slots.at[d], send.at[d], recv.at[d], p) for d, p in enumerate(peers)]


def begin(copies):
    for copy in copies:
        copy.start()


def finish(copies):
    for copy in copies:
        copy.wait()


def step_kernel(
    groups, devs, count_ref, own_ref, flat_ref, out_ref,
    held, flat, outgoing, joined, mine, u_ref, plo, phi,
    count_msg, row_msg, count_row, count_col, total_ref, small_ref, top_ref,
    crow_send, crow_recv, ccol_send, ccol_recv, block_sem, local_sem,
    w_ref, sx_ref, fx_ref, acc_ref, one_ref, edge_lo, edge_hi, plo2, phi2,
    xlo, xhi, glo, ghi, xlo2, xhi2, glo2, ghi2, ly, ry, fy, lz, rz, fz,
    speed_msg, speed_row, speed_col, step_ref,
    row_send, row_recv, col_send, col_recv, send, recv, send2, recv2,
):
    staged = pltpu.make_async_copy(own_ref, held, local_sem.at[0])
    staged.start()
    g, j, me, curve_next, curve_prev, row, column = ring(groups, devs)
    greet(row + column + [curve_next, curve_prev])
    up = (lax.rem(g + 1, groups), j)
    down = (lax.rem(g + groups - 1, groups), j)
    right = (g, lax.rem(j + 1, devs))
    left = (g, lax.rem(j + devs - 1, devs))
    speeds = messages(top_ref, speed_row, row_send, row_recv, row)
    rebalance(
        g, j, me, groups * devs, curve_next, count_ref, own_ref, flat_ref, held, flat, outgoing,
        joined, mine, u_ref, plo, phi, count_msg, row_msg, count_row, count_col, total_ref,
        small_ref, top_ref, row, column, crow_send, crow_recv, ccol_send, ccol_recv, speeds,
        block_sem, local_sem, staged,
    )
    y_copies = [
        remote(phi, glo, send.at[2], recv.at[2], right),
        remote(plo, ghi, send.at[3], recv.at[3], left),
    ]
    begin(y_copies)
    x_copies = [
        remote(u_ref.at[pl.ds(BS - 2, 2)], xlo, send.at[0], recv.at[0], up),
        remote(u_ref.at[pl.ds(0, 2)], xhi, send.at[1], recv.at[1], down),
    ]
    begin(x_copies)

    fill_planes(u_ref, w_ref, 2)
    z_pass(w_ref, acc_ref, lz, rz, fz)

    finish(speeds)
    top = top_ref[...]
    for d in range(devs - 1):
        top = jnp.maximum(top, speed_row[d])
    speed_msg[...] = top
    speeds = messages(speed_msg, speed_col, col_send, col_recv, column)
    begin(speeds)

    finish(y_copies)
    fill_ghosts(glo, ghi, w_ref)
    y_pass(w_ref, acc_ref, ly, ry, fy)
    finish(x_copies)
    fill_planes(xlo, w_ref, 0)
    fill_planes(xhi, w_ref, BS + 2)
    x_faces(w_ref, sx_ref, fx_ref)

    finish(speeds)
    top = speed_msg[...]
    for d in range(groups - 1):
        top = jnp.maximum(top, speed_col[d])
    top = jnp.max(jnp.max(top, axis=1, keepdims=True), axis=0, keepdims=True)
    step_ref[...] = COURANT / jnp.broadcast_to(top, (8, LANES))

    def update(c, edge, place):
        step = step_ref[...]
        low, high = [], []
        for f in range(FIELDS):
            change = (fx_ref[c + 1, f] - fx_ref[c, f]) + acc_ref[c, f]
            new = u_ref[c, f] - step * change
            one_ref[c, f] = new
            if edge is not None:
                edge[place, f] = new
            low.append(new[0])
            high.append(new[YV - 1])
        for q, tile in enumerate(pack(low, 0)):
            plo2[c, q] = tile
        for q, tile in enumerate(pack(high, 96)):
            phi2[c, q] = tile

    def middle(c, carry):
        update(c, None, 0)
        return carry

    for place in range(2):
        update(place, edge_lo, place)
        update(BS - 2 + place, edge_hi, place)
    x_copies = [
        remote(edge_hi, xlo2, send2.at[0], recv2.at[0], up),
        remote(edge_lo, xhi2, send2.at[1], recv2.at[1], down),
    ]
    begin(x_copies)
    lax.fori_loop(2, BS - 2, middle, 0)
    y_copies = [
        remote(phi2, glo2, send2.at[2], recv2.at[2], right),
        remote(plo2, ghi2, send2.at[3], recv2.at[3], left),
    ]
    begin(y_copies)

    fill_planes(one_ref, w_ref, 2)
    z_pass(w_ref, acc_ref, lz, rz, fz)
    finish(y_copies)
    fill_ghosts(glo2, ghi2, w_ref)
    y_pass(w_ref, acc_ref, ly, ry, fy)
    finish(x_copies)
    fill_planes(xlo2, w_ref, 0)
    fill_planes(xhi2, w_ref, BS + 2)
    x_faces(w_ref, sx_ref, fx_ref)

    def last(c, carry):
        step = step_ref[...]
        for f in range(FIELDS):
            change = (fx_ref[c + 1, f] - fx_ref[c, f]) + acc_ref[c, f]
            new = 0.5 * (u_ref[c, f] + one_ref[c, f] - step * change)
            for v in range(YV):
                row = (v // 2) * (BRICK_Z * ROWS) + (c * 2 + v % 2) * FIELDS + f
                out_ref[pl.ds(row, BRICK_Z, stride=ROWS), :] = new[v]
        return carry

    lax.fori_loop(0, BS, last, 0)


def signal_speed(u):
    w, inverse = primitive(u)
    b2 = [w[5 + i] * w[5 + i] for i in range(3)]
    sound = GAMMA * w[4] * inverse
    alfven = (b2[0] + b2[1] + b2[2]) * inverse
    speeds = [jnp.abs(w[1 + i]) + fast_from(sound, alfven, b2[i] * inverse) for i in range(3)]
    return jnp.maximum(jnp.maximum(speeds[0], speeds[1]), speeds[2])


def rebalance(
    g, j, me, total, curve_next, count_ref, own_ref, flat_ref, held, flat, outgoing, joined,
    mine, u_ref, plo, phi, count_msg, row_msg, count_row, count_col, total_ref, small_ref, top_ref,
    row, column, crow_send, crow_recv, ccol_send, ccol_recv, speeds, block_sem, local_sem, staged,
):
    cap = own_ref.shape[0]
    count = count_ref[0]
    count_msg[...] = jnp.full((8, LANES), count, jnp.int32)
    counts = messages(count_msg, count_row, crow_send, crow_recv, row)
    begin(counts)
    staged.wait()

    def stage(m, carry):
        outgoing[m] = held[jnp.clip(count - BLK_DEV + 1 + m, 0, cap - 1)]
        return carry

    lax.fori_loop(0, BLK_DEV - 1, stage, 0)
    blocks = remote(
        outgoing, joined.at[pl.ds(1, BLK_DEV - 1)], block_sem.at[0], block_sem.at[1], curve_next
    )

    @pl.when(me < total - 1)
    def _():
        blocks.start()

    spare = pltpu.make_async_copy(flat_ref, flat, local_sem.at[1])
    spare.start()
    local = pltpu.make_async_copy(
        own_ref.at[pl.ds(0, BLK_DEV)], joined.at[pl.ds(BLK_DEV, BLK_DEV)], local_sem.at[2]
    )
    local.start()

    finish(counts)
    before = jnp.zeros((8, LANES), jnp.int32)
    every = count_msg[...]
    for d in range(1, len(row) + 1):
        value = count_row[d - 1]
        every = every + value
        before = before + jnp.where(d <= j, value, 0)
    row_msg[...] = every
    counts = messages(row_msg, count_col, ccol_send, ccol_recv, column)
    begin(counts)

    spare.wait()
    slot = lax.broadcasted_iota(jnp.int32, (8, LANES), 0)

    def chunk(t, top):
        for first in list(range(0, cap - 8, 8)) + [cap - 8]:
            u = [
                flat[pl.ds(first * ROWS + t * FIELDS + f, 8, stride=ROWS), :]
                for f in range(FIELDS)
            ]
            top = jnp.maximum(top, jnp.where(slot + first < count, signal_speed(u), 0.0))
        return top

    top_ref[...] = lax.fori_loop(0, CHUNKS, chunk, jnp.zeros((8, LANES), jnp.float32))
    begin(speeds)

    finish(counts)
    for d in range(1, len(column) + 1):
        before = before + jnp.where(d <= g, count_col[d - 1], 0)
    total_ref[...] = before - me * BLK_DEV
    narrow = pltpu.make_async_copy(total_ref, small_ref, local_sem.at[3])
    narrow.start()
    narrow.wait()
    surplus = jnp.clip(small_ref[0, 0], 0, BLK_DEV - 1)
    local.wait()

    @pl.when(me < total - 1)
    def _():
        blocks.wait_send()

    @pl.when(me > 0)
    def _():
        blocks.wait_recv()

    def take(k, carry):
        mine[pl.ds(pl.multiple_of(k * ROWS, ROWS), ROWS), :] = joined[BLK_DEV - surplus + k]
        return carry

    lax.fori_loop(0, BLK_DEV, take, 0)

    def assemble(c, carry):
        for v in range(YV):
            for f in range(FIELDS):
                base = (v // 2) * BRICK_Z * ROWS
                u_ref[c, f, v] = mine[
                    pl.ds(base + (c * 2 + v % 2) * FIELDS + f, BRICK_Z, stride=ROWS), :
                ]
        for q, tile in enumerate(pack([u_ref[c, f, 0] for f in range(FIELDS)], 0)):
            plo[c, q] = tile
        for q, tile in enumerate(pack([u_ref[c, f, YV - 1] for f in range(FIELDS)], 96)):
            phi[c, q] = tile
        return carry

    lax.fori_loop(0, BS, assemble, 0)


TILE = (8, LANES)
SLAB = (BS, FIELDS, YV) + TILE
EDGE = (2, FIELDS, YV) + TILE
PACK = (BS, 2) + TILE
LIMIT = 60 * 1024 * 1024


def f32(*shape):
    return jax.ShapeDtypeStruct(shape, jnp.float32)


VMEM = pl.BlockSpec(memory_space=pltpu.VMEM)
ANY = pl.BlockSpec(memory_space=pl.ANY)
SMEM = pl.BlockSpec(memory_space=pltpu.SMEM)


def body(groups, devs, blocks_in, counts):
    cap = blocks_in.shape[0]
    rows = blocks_in.reshape(cap, FIELDS, CHUNKS, LANES).transpose(0, 2, 1, 3)
    rows = rows.reshape(cap, ROWS, LANES)
    dma = pltpu.SemaphoreType.DMA

    def vmem(*shape):
        return pltpu.VMEM(shape, jnp.float32)

    ghosts = [vmem(*EDGE), vmem(*EDGE), vmem(*PACK), vmem(*PACK)]
    out = pl.pallas_call(
        functools.partial(step_kernel, groups, devs),
        out_shape=f32(BLK_DEV * ROWS, LANES),
        in_specs=[SMEM, ANY, ANY],
        out_specs=VMEM,
        scratch_shapes=[
            vmem(cap, ROWS, LANES),
            vmem(cap * ROWS, LANES),
            vmem(BLK_DEV - 1, ROWS, LANES),
            vmem(2 * BLK_DEV, ROWS, LANES),
            vmem(BLK_DEV * ROWS, LANES),
            vmem(*SLAB), vmem(*PACK), vmem(*PACK),
            pltpu.VMEM(TILE, jnp.int32),
            pltpu.VMEM(TILE, jnp.int32),
            pltpu.VMEM((devs - 1,) + TILE, jnp.int32),
            pltpu.VMEM((groups - 1,) + TILE, jnp.int32),
            pltpu.VMEM(TILE, jnp.int32),
            pltpu.SMEM(TILE, jnp.int32),
            vmem(*TILE),
            dma((devs - 1,)), dma((devs - 1,)), dma((groups - 1,)), dma((groups - 1,)),
            dma((2,)), dma((4,)),
            vmem(BS + 4, FIELDS, YV + 2, *TILE),
            vmem(BS + 2, FIELDS, YV, *TILE),
            vmem(BS + 1, FIELDS, YV, *TILE),
            vmem(*SLAB),
            vmem(*SLAB),
        ] + ghosts + ghosts + ghosts + [vmem(FIELDS, YV + 1, *TILE)] * 3
        + [vmem(FIELDS, YV, *TILE)] * 3 + [
            vmem(*TILE), vmem(devs - 1, *TILE), vmem(groups - 1, *TILE), vmem(*TILE),
            dma((devs - 1,)), dma((devs - 1,)), dma((groups - 1,)), dma((groups - 1,)),
            dma((4,)), dma((4,)), dma((4,)), dma((4,)),
        ],
        compiler_params=pltpu.CompilerParams(
            collective_id=0, has_side_effects=True, vmem_limit_bytes=LIMIT
        ),
        name="step",
    )(counts, rows, rows.reshape(cap * ROWS, LANES))
    out = out.reshape(BLK_DEV, CHUNKS, FIELDS, LANES).transpose(0, 2, 1, 3)
    return out.reshape(BLK_DEV, FIELDS, CHUNKS * LANES)


def solution(mesh):
    groups, devs = mesh.shape["group"], mesh.shape["dev"]
    in_specs = (P(("group", "dev"), None, None), P(("group", "dev")))
    out_specs = P(("group", "dev"), None, None)
    return jax.shard_map(
        functools.partial(body, groups, devs),
        mesh=mesh, in_specs=in_specs, out_specs=out_specs, check_vma=False,
    )
```

```python
import functools

import jax
import jax.numpy as jnp
from jax import lax
from jax.experimental import pallas as pl
from jax.experimental.pallas import tpu as pltpu
from jax.sharding import PartitionSpec as P

BS = 16
BRICK_Y = 2
BRICK_Z = 8
BLK_DEV = 16
FIELDS = 8
LANES = 128
CHUNKS = 32
ROWS = CHUNKS * FIELDS
YV = 4

GAMMA = 5.0 / 3.0
COURANT = 0.25
DENSITY_FLOOR = 0.05
PRESSURE_FLOOR = 0.05
TINY = 1.2e-38

MESH = pl.DeviceIdType.MESH


def reciprocal(x):
    guess = pl.reciprocal(x, approx=True)
    return guess * (2.0 - x * guess)


def primitive(u):
    density = jnp.maximum(u[0], DENSITY_FLOOR)
    inverse = reciprocal(density)
    vx, vy, vz = u[1] * inverse, u[2] * inverse, u[3] * inverse
    kinetic = 0.5 * density * (vx * vx + vy * vy + vz * vz)
    energy_b = 0.5 * (u[5] * u[5] + u[6] * u[6] + u[7] * u[7])
    pressure = jnp.maximum((GAMMA - 1.0) * (u[4] - kinetic - energy_b), PRESSURE_FLOOR)
    return [density, vx, vy, vz, pressure, u[5], u[6], u[7]], inverse


def fast_from(sound, alfven, along):
    total = sound + alfven
    inner = jnp.maximum(total * total - 4.0 * sound * along, TINY)
    outer = 0.5 * (total + inner * lax.rsqrt(inner))
    return outer * lax.rsqrt(outer)


def wave(w, n):
    inverse = reciprocal(w[0])
    b2 = w[5] * w[5] + w[6] * w[6] + w[7] * w[7]
    bn = w[5 + n]
    return fast_from(GAMMA * w[4] * inverse, b2 * inverse, bn * bn * inverse), 0.5 * b2


def weighted(w, half_b2, n, weight, shift):
    r, v, p, b = w[0], w[1:4], w[4], w[5:8]
    vn, bn = v[n], b[n]
    k = weight * vn + shift
    q = r * k
    wb = weight * bn
    wp = weight * (p + half_b2)
    energy = p * (1.0 / (GAMMA - 1.0)) + half_b2 + 0.5 * r * (v[0] * v[0] + v[1] * v[1] + v[2] * v[2])
    vb = v[0] * b[0] + v[1] * b[1] + v[2] * b[2]
    momentum = [v[i] * q - b[i] * wb for i in range(3)]
    momentum[n] = momentum[n] + wp
    field = [shift * bn if i == n else b[i] * k - v[i] * wb for i in range(3)]
    return [q] + momentum + [energy * k + wp * vn - wb * vb] + field


def hlle(left, right, n):
    cl, hl = wave(left, n)
    cr, hr = wave(right, n)
    vl, vr = left[1 + n], right[1 + n]
    upper = jnp.maximum(jnp.maximum(vr + cr, vl + cl), 0.0)
    lower = jnp.minimum(jnp.minimum(vl - cl, vr - cr), 0.0)
    inverse = reciprocal(upper - lower)
    a = upper * inverse
    c = a * lower
    first = weighted(left, hl, n, a, -c)
    second = weighted(right, hr, n, -lower * inverse, c)
    return [x + y for x, y in zip(first, second)]


def half_minmod(a, b):
    return 0.5 * (jnp.maximum(jnp.minimum(a, b), 0.0) + jnp.minimum(jnp.maximum(a, b), 0.0))


def roll(x, shift, axis):
    size = x.shape[axis]
    shift = shift % size
    return x if shift == 0 else pltpu.roll(x, shift, axis)


def lane_index():
    return lax.broadcasted_iota(jnp.int32, (8, LANES), 1)


def lane_gather(x, index):
    return jnp.take_along_axis(x, index, axis=1, mode="promise_in_bounds")


def z_up(tiles):
    lane = lane_index()
    edge = lane % BS == 0
    index = lane - lane % BS + (lane + 1) % BS
    moved = [jnp.where(edge, roll(x, -1, 0), x) for x in tiles]
    return jnp.stack([lane_gather(x, index) for x in moved])


def z_down(tiles):
    lane = lane_index()
    edge = lane % BS == BS - 1
    index = lane - lane % BS + (lane + BS - 1) % BS
    moved = [jnp.where(edge, roll(x, 1, 0), x) for x in tiles]
    return jnp.stack([lane_gather(x, index) for x in moved])


def split(x):
    return [x[i] for i in range(x.shape[0])]


def fill_planes(source, w_ref, base, v=0, n=YV):
    def one(c, carry):
        w, _ = primitive([source[c, f, v:v + n] for f in range(FIELDS)])
        for f in range(FIELDS):
            w_ref[base + c, f, 1 + v:1 + v + n] = w[f]
        return carry

    lax.fori_loop(0, source.shape[0], one, 0)


def fill_ghosts(glo_ref, ghi_ref, w_ref):
    def one(c, carry):
        for ghost, v, base in ((glo_ref, 0, 96), (ghi_ref, YV + 1, 0)):
            u = [roll(ghost[c, f // 4], base - 32 * (f % 4), 1) for f in range(FIELDS)]
            w, _ = primitive(u)
            for f in range(FIELDS):
                w_ref[c + 2, f, v] = w[f]
        return carry

    lax.fori_loop(0, BS, one, 0)


PAIRS = ((0, 2), (2, 2))


def x_faces(w_ref, sx_ref, fx_ref):
    def slopes(c, carry):
        for f in range(FIELDS):
            here = w_ref[c + 1, f, 1:YV + 1]
            sx_ref[c, f] = half_minmod(
                here - w_ref[c, f, 1:YV + 1], w_ref[c + 2, f, 1:YV + 1] - here
            )
        return carry

    lax.fori_loop(0, BS + 2, slopes, 0)

    def one(face, carry):
        for v, n in PAIRS:
            left = [w_ref[face + 1, f, v + 1:v + 1 + n] + sx_ref[face, f, v:v + n] for f in range(FIELDS)]
            right = [
                w_ref[face + 2, f, v + 1:v + 1 + n] - sx_ref[face + 1, f, v:v + n]
                for f in range(FIELDS)
            ]
            for f, flux in enumerate(hlle(left, right, 0)):
                fx_ref[face, f, v:v + n] = flux
        return carry

    lax.fori_loop(0, BS + 1, one, 0)


def faces(l_ref, r_ref, f_ref, n, parts):
    for v, size in parts:
        left = [l_ref[f, v:v + size] for f in range(FIELDS)]
        right = [r_ref[f, v:v + size] for f in range(FIELDS)]
        for f, flux in enumerate(hlle(left, right, n)):
            f_ref[f, v:v + size] = flux


def y_faces(w_ref, c, l_ref, r_ref, f_ref):
    lane = lax.broadcasted_iota(jnp.int32, (YV + 2, 8, LANES), 2)
    top = lane >= LANES - BS
    bottom = lane < BS
    for f in range(FIELDS):
        w = w_ref[c + 2, f]
        rolled = roll(w, -BS, 2)
        diff = jnp.where(top, jnp.concatenate([rolled[1:], rolled[-1:]]), rolled) - w
        rolled = roll(diff, BS, 2)
        down = jnp.where(bottom, jnp.concatenate([rolled[:1], rolled[:-1]]), rolled)
        slope = half_minmod(down, diff)
        low = roll(w - slope, -BS, 2)
        l_ref[f] = (w + slope)[:YV + 1]
        r_ref[f] = jnp.where(top[1:], low[1:], low[:-1])
    faces(l_ref, r_ref, f_ref, 1, PAIRS + ((YV, 1),))


def z_faces(w_ref, c, l_ref, r_ref, f_ref, v, n):
    for f in range(FIELDS):
        w = w_ref[c + 2, f, 1 + v:1 + v + n]
        diff = z_up(split(w)) - w
        slope = half_minmod(z_down(split(diff)), diff)
        l_ref[f, v:v + n] = w + slope
        r_ref[f, v:v + n] = z_up(split(w - slope))
    faces(l_ref, r_ref, f_ref, 2, [(i, 2) for i in range(v, v + n, 2)])


def z_pass(w_ref, acc_ref, lz, rz, fz, v=0, n=YV):
    def one(c, carry):
        z_faces(w_ref, c, lz, rz, fz, v, n)
        for f in range(FIELDS):
            flux = fz[f, v:v + n]
            acc_ref[c, f, v:v + n] = flux - z_down(split(flux))
        return carry

    lax.fori_loop(0, BS, one, 0)


def y_pass(w_ref, acc_ref, ly, ry, fy):
    bottom = lax.broadcasted_iota(jnp.int32, (YV, 8, LANES), 2) < BS

    def one(c, carry):
        y_faces(w_ref, c, ly, ry, fy)
        for f in range(FIELDS):
            flux = fy[f]
            rolled = roll(flux, BS, 2)
            across = flux[1:] - jnp.where(bottom, rolled[:-1], rolled[1:])
            acc_ref[c, f] = across + acc_ref[c, f]
        return carry

    lax.fori_loop(0, BS, one, 0)


def pack(tiles, base):
    group = lane_index() // 32
    out = []
    for q in range(2):
        total = roll(tiles[4 * q], -base, 1)
        for k in range(1, 4):
            total = jnp.where(group == k, roll(tiles[4 * q + k], 32 * k - base, 1), total)
        out.append(total)
    return out


def ring(groups, devs):
    g, j = lax.axis_index("group"), lax.axis_index("dev")
    me = g * devs + j
    count = groups * devs
    after, before = lax.rem(me + 1, count), lax.rem(me + count - 1, count)
    curve_next = (after // devs, lax.rem(after, devs))
    curve_prev = (before // devs, lax.rem(before, devs))
    row = [(g, lax.rem(j + d, devs)) for d in range(1, devs)]
    column = [(lax.rem(g + d, groups), j) for d in range(1, groups)]
    return g, j, me, curve_next, curve_prev, row, column


def greet(peers):
    barrier = pltpu.get_barrier_semaphore()
    for peer in peers:
        pl.semaphore_signal(barrier, inc=1, device_id=peer, device_id_type=MESH)
    pl.semaphore_wait(barrier, len(peers))


def remote(source, target, send, recv, device):
    return pltpu.make_async_remote_copy(
        src_ref=source, dst_ref=target, send_sem=send, recv_sem=recv,
        device_id=device, device_id_type=MESH,
    )


def messages(source, slots, send, recv, peers):
    return [remote(source, slots.at[d], send.at[d], recv.at[d], p) for d, p in enumerate(peers)]


def begin(copies):
    for copy in copies:
        copy.start()


def finish(copies):
    for copy in copies:
        copy.wait()


def step_kernel(
    groups, devs, count_ref, own_ref, flat_ref, out_ref,
    held, flat, outgoing, joined_lo, joined_hi, mine, u_ref, plo, phi,
    count_msg, row_msg, count_row, count_col, total_ref, small_ref, top_ref,
    crow_send, crow_recv, ccol_send, ccol_recv, block_sem, local_sem,
    w_ref, sx_ref, fx_ref, acc_ref, one_ref, edge_lo, edge_hi, plo2, phi2,
    xlo, xhi, glo, ghi, xlo2, xhi2, glo2, ghi2, ly, ry, fy, lz, rz, fz,
    speed_msg, speed_row, speed_col, step_ref,
    row_send, row_recv, col_send, col_recv, send, recv, send2, recv2,
):
    staged = pltpu.make_async_copy(own_ref, held, local_sem.at[0])
    staged.start()
    g, j, me, curve_next, curve_prev, row, column = ring(groups, devs)
    greet(row + column + [curve_next, curve_prev])
    up = (lax.rem(g + 1, groups), j)
    down = (lax.rem(g + groups - 1, groups), j)
    right = (g, lax.rem(j + 1, devs))
    left = (g, lax.rem(j + devs - 1, devs))
    speeds = messages(top_ref, speed_row, row_send, row_recv, row)
    rebalance(
        g, j, me, groups * devs, curve_next, count_ref, own_ref, flat_ref, held, flat, outgoing,
        joined_lo, joined_hi, mine, u_ref, plo, phi, count_msg, row_msg, count_row, count_col, total_ref,
        small_ref, top_ref, row, column, crow_send, crow_recv, ccol_send, ccol_recv, speeds,
        block_sem, local_sem, staged, w_ref, acc_ref, lz, rz, fz,
    )
    y_copies = [
        remote(phi, glo, send.at[2], recv.at[2], right),
        remote(plo, ghi, send.at[3], recv.at[3], left),
    ]
    begin(y_copies)
    x_copies = [
        remote(u_ref.at[pl.ds(BS - 2, 2)], xlo, send.at[0], recv.at[0], up),
        remote(u_ref.at[pl.ds(0, 2)], xhi, send.at[1], recv.at[1], down),
    ]
    begin(x_copies)

    fill_planes(u_ref, w_ref, 2, 0, 2)
    z_pass(w_ref, acc_ref, lz, rz, fz, 0, 2)

    finish(speeds)
    top = top_ref[...]
    for d in range(devs - 1):
        top = jnp.maximum(top, speed_row[d])
    speed_msg[...] = top
    speeds = messages(speed_msg, speed_col, col_send, col_recv, column)
    begin(speeds)

    finish(y_copies)
    fill_ghosts(glo, ghi, w_ref)
    y_pass(w_ref, acc_ref, ly, ry, fy)
    finish(x_copies)
    fill_planes(xlo, w_ref, 0)
    fill_planes(xhi, w_ref, BS + 2)
    x_faces(w_ref, sx_ref, fx_ref)

    finish(speeds)
    top = speed_msg[...]
    for d in range(groups - 1):
        top = jnp.maximum(top, speed_col[d])
    top = jnp.max(jnp.max(top, axis=1, keepdims=True), axis=0, keepdims=True)
    step_ref[...] = COURANT / jnp.broadcast_to(top, (8, LANES))

    def update(c, edge, place):
        step = step_ref[...]
        low, high = [], []
        for f in range(FIELDS):
            change = (fx_ref[c + 1, f] - fx_ref[c, f]) + acc_ref[c, f]
            new = u_ref[c, f] - step * change
            one_ref[c, f] = new
            if edge is not None:
                edge[place, f] = new
            low.append(new[0])
            high.append(new[YV - 1])
        for q, tile in enumerate(pack(low, 0)):
            plo2[c, q] = tile
        for q, tile in enumerate(pack(high, 96)):
            phi2[c, q] = tile

    def middle(c, carry):
        update(c, None, 0)
        return carry

    for place in range(2):
        update(place, edge_lo, place)
        update(BS - 2 + place, edge_hi, place)
    x_copies = [
        remote(edge_hi, xlo2, send2.at[0], recv2.at[0], up),
        remote(edge_lo, xhi2, send2.at[1], recv2.at[1], down),
    ]
    begin(x_copies)
    lax.fori_loop(2, BS - 2, middle, 0)
    y_copies = [
        remote(phi2, glo2, send2.at[2], recv2.at[2], right),
        remote(plo2, ghi2, send2.at[3], recv2.at[3], left),
    ]
    begin(y_copies)

    fill_planes(one_ref, w_ref, 2)
    z_pass(w_ref, acc_ref, lz, rz, fz)
    finish(y_copies)
    fill_ghosts(glo2, ghi2, w_ref)
    y_pass(w_ref, acc_ref, ly, ry, fy)
    finish(x_copies)
    fill_planes(xlo2, w_ref, 0)
    fill_planes(xhi2, w_ref, BS + 2)
    x_faces(w_ref, sx_ref, fx_ref)

    def last(c, carry):
        step = step_ref[...]
        for f in range(FIELDS):
            change = (fx_ref[c + 1, f] - fx_ref[c, f]) + acc_ref[c, f]
            new = 0.5 * (u_ref[c, f] + one_ref[c, f] - step * change)
            for v in range(YV):
                row = (v // 2) * (BRICK_Z * ROWS) + (c * 2 + v % 2) * FIELDS + f
                out_ref[pl.ds(row, BRICK_Z, stride=ROWS), :] = new[v]
        return carry

    lax.fori_loop(0, BS, last, 0)


def signal_speed(u):
    w, inverse = primitive(u)
    b2 = [w[5 + i] * w[5 + i] for i in range(3)]
    sound = GAMMA * w[4] * inverse
    alfven = (b2[0] + b2[1] + b2[2]) * inverse
    speeds = [jnp.abs(w[1 + i]) + fast_from(sound, alfven, b2[i] * inverse) for i in range(3)]
    return jnp.maximum(jnp.maximum(speeds[0], speeds[1]), speeds[2])


def rebalance(
    g, j, me, total, curve_next, count_ref, own_ref, flat_ref, held, flat, outgoing, joined_lo, joined_hi,
    mine, u_ref, plo, phi, count_msg, row_msg, count_row, count_col, total_ref, small_ref, top_ref,
    row, column, crow_send, crow_recv, ccol_send, ccol_recv, speeds, block_sem, local_sem, staged,
    w_ref, acc_ref, lz, rz, fz,
):
    cap = own_ref.shape[0]
    count = count_ref[0]
    count_msg[...] = jnp.full((8, LANES), count, jnp.int32)
    counts = messages(count_msg, count_row, crow_send, crow_recv, row)
    begin(counts)
    staged.wait()

    def stage(m, carry):
        outgoing[m] = held[jnp.clip(count - BLK_DEV + 1 + m, 0, cap - 1)]
        return carry

    lax.fori_loop(0, BLK_DEV - 1, stage, 0)
    early, late = BLK_DEV - BRICK_Z - 1, BRICK_Z
    upper = remote(
        outgoing.at[pl.ds(late, early)], joined_hi.at[pl.ds(0, early)],
        block_sem.at[0], block_sem.at[1], curve_next,
    )
    lower = remote(
        outgoing.at[pl.ds(0, late)], joined_lo.at[pl.ds(0, late)],
        block_sem.at[2], block_sem.at[3], curve_next,
    )

    @pl.when(me < total - 1)
    def _():
        upper.start()
        lower.start()

    spare = pltpu.make_async_copy(flat_ref, flat, local_sem.at[1])
    spare.start()
    local_hi = pltpu.make_async_copy(
        own_ref.at[pl.ds(0, BLK_DEV)], joined_hi.at[pl.ds(early, BLK_DEV)], local_sem.at[2]
    )
    local_hi.start()
    local_lo = pltpu.make_async_copy(
        own_ref.at[pl.ds(0, BRICK_Z)], joined_lo.at[pl.ds(late + early, BRICK_Z)], local_sem.at[4]
    )
    local_lo.start()

    finish(counts)
    before = jnp.zeros((8, LANES), jnp.int32)
    every = count_msg[...]
    for d in range(1, len(row) + 1):
        value = count_row[d - 1]
        every = every + value
        before = before + jnp.where(d <= j, value, 0)
    row_msg[...] = every
    counts = messages(row_msg, count_col, ccol_send, ccol_recv, column)
    begin(counts)

    spare.wait()
    slot = lax.broadcasted_iota(jnp.int32, (8, LANES), 0)

    def chunk(t, top):
        for first in list(range(0, cap - 8, 8)) + [cap - 8]:
            u = [
                flat[pl.ds(first * ROWS + t * FIELDS + f, 8, stride=ROWS), :]
                for f in range(FIELDS)
            ]
            top = jnp.maximum(top, jnp.where(slot + first < count, signal_speed(u), 0.0))
        return top

    top_ref[...] = lax.fori_loop(0, CHUNKS, chunk, jnp.zeros((8, LANES), jnp.float32))
    begin(speeds)

    finish(counts)
    for d in range(1, len(column) + 1):
        before = before + jnp.where(d <= g, count_col[d - 1], 0)
    total_ref[...] = before - me * BLK_DEV
    narrow = pltpu.make_async_copy(total_ref, small_ref, local_sem.at[3])
    narrow.start()
    narrow.wait()
    surplus = jnp.clip(small_ref[0, 0], 0, BLK_DEV - 1)
    first = BLK_DEV - 1 - surplus

    def take(joined, half):
        def one(k, carry):
            mine[half, pl.ds(pl.multiple_of(k * ROWS, ROWS), ROWS), :] = joined[first + k]
            return carry

        lax.fori_loop(0, BRICK_Z, one, 0)

        def assemble(c, carry):
            for v in (2 * half, 2 * half + 1):
                for f in range(FIELDS):
                    u_ref[c, f, v] = mine[
                        half, pl.ds((c * 2 + v % 2) * FIELDS + f, BRICK_Z, stride=ROWS), :
                    ]
            side, edge, target = ((0, 0, plo), (YV - 1, 96, phi))[half]
            for q, tile in enumerate(pack([u_ref[c, f, side] for f in range(FIELDS)], edge)):
                target[c, q] = tile
            return carry

        lax.fori_loop(0, BS, assemble, 0)

    local_hi.wait()

    @pl.when(me < total - 1)
    def _():
        upper.wait_send()

    @pl.when(me > 0)
    def _():
        upper.wait_recv()

    shared = pltpu.make_async_copy(
        joined_hi.at[pl.ds(0, early)], joined_lo.at[pl.ds(late, early)], local_sem.at[5]
    )
    shared.start()
    take(joined_hi, 1)
    fill_planes(u_ref, w_ref, 2, 2, 2)
    z_pass(w_ref, acc_ref, lz, rz, fz, 2, 2)

    local_lo.wait()
    shared.wait()

    @pl.when(me < total - 1)
    def _():
        lower.wait_send()

    @pl.when(me > 0)
    def _():
        lower.wait_recv()

    take(joined_lo, 0)


TILE = (8, LANES)
SLAB = (BS, FIELDS, YV) + TILE
EDGE = (2, FIELDS, YV) + TILE
PACK = (BS, 2) + TILE
LIMIT = 51 * 1024 * 1024


def f32(*shape):
    return jax.ShapeDtypeStruct(shape, jnp.float32)


VMEM = pl.BlockSpec(memory_space=pltpu.VMEM)
ANY = pl.BlockSpec(memory_space=pl.ANY)
SMEM = pl.BlockSpec(memory_space=pltpu.SMEM)


def body(groups, devs, blocks_in, counts):
    cap = blocks_in.shape[0]
    rows = blocks_in.reshape(cap, FIELDS, CHUNKS, LANES).transpose(0, 2, 1, 3)
    rows = rows.reshape(cap, ROWS, LANES)
    dma = pltpu.SemaphoreType.DMA

    def vmem(*shape):
        return pltpu.VMEM(shape, jnp.float32)

    ghosts = [vmem(*EDGE), vmem(*EDGE), vmem(*PACK), vmem(*PACK)]
    out = pl.pallas_call(
        functools.partial(step_kernel, groups, devs),
        out_shape=f32(BLK_DEV * ROWS, LANES),
        in_specs=[SMEM, ANY, ANY],
        out_specs=VMEM,
        scratch_shapes=[
            vmem(cap, ROWS, LANES),
            vmem(cap * ROWS, LANES),
            vmem(BLK_DEV - 1, ROWS, LANES),
            vmem(BLK_DEV + BRICK_Z - 1, ROWS, LANES),
            vmem(BLK_DEV + BRICK_Z - 1, ROWS, LANES),
            vmem(2, BRICK_Z * ROWS, LANES),
            vmem(*SLAB), vmem(*PACK), vmem(*PACK),
            pltpu.VMEM(TILE, jnp.int32),
            pltpu.VMEM(TILE, jnp.int32),
            pltpu.VMEM((devs - 1,) + TILE, jnp.int32),
            pltpu.VMEM((groups - 1,) + TILE, jnp.int32),
            pltpu.VMEM(TILE, jnp.int32),
            pltpu.SMEM(TILE, jnp.int32),
            vmem(*TILE),
            dma((devs - 1,)), dma((devs - 1,)), dma((groups - 1,)), dma((groups - 1,)),
            dma((4,)), dma((6,)),
            vmem(BS + 4, FIELDS, YV + 2, *TILE),
            vmem(BS + 2, FIELDS, YV, *TILE),
            vmem(BS + 1, FIELDS, YV, *TILE),
            vmem(*SLAB),
            vmem(*SLAB),
        ] + ghosts + ghosts + ghosts + [vmem(FIELDS, YV + 1, *TILE)] * 3
        + [vmem(FIELDS, YV, *TILE)] * 3 + [
            vmem(*TILE), vmem(devs - 1, *TILE), vmem(groups - 1, *TILE), vmem(*TILE),
            dma((devs - 1,)), dma((devs - 1,)), dma((groups - 1,)), dma((groups - 1,)),
            dma((4,)), dma((4,)), dma((4,)), dma((4,)),
        ],
        compiler_params=pltpu.CompilerParams(
            collective_id=0, has_side_effects=True, vmem_limit_bytes=LIMIT
        ),
        name="step",
    )(counts, rows, rows.reshape(cap * ROWS, LANES))
    out = out.reshape(BLK_DEV, CHUNKS, FIELDS, LANES).transpose(0, 2, 1, 3)
    return out.reshape(BLK_DEV, FIELDS, CHUNKS * LANES)


def solution(mesh):
    groups, devs = mesh.shape["group"], mesh.shape["dev"]
    in_specs = (P(("group", "dev"), None, None), P(("group", "dev")))
    out_specs = P(("group", "dev"), None, None)
    return jax.shard_map(
        functools.partial(body, groups, devs),
        mesh=mesh, in_specs=in_specs, out_specs=out_specs, check_vma=False,
    )
```

```python
import functools

import jax
import jax.numpy as jnp
from jax import lax
from jax.experimental import pallas as pl
from jax.experimental.pallas import tpu as pltpu
from jax.sharding import PartitionSpec as P

BS = 16
BRICK_Y = 2
BRICK_Z = 8
BLK_DEV = 16
FIELDS = 8
LANES = 128
CHUNKS = 32
ROWS = CHUNKS * FIELDS
YV = 4

GAMMA = 5.0 / 3.0
COURANT = 0.25
DENSITY_FLOOR = 0.05
PRESSURE_FLOOR = 0.05
TINY = 1.2e-38

MESH = pl.DeviceIdType.MESH


def reciprocal(x):
    guess = pl.reciprocal(x, approx=True)
    return guess * (2.0 - x * guess)


def primitive(u):
    density = jnp.maximum(u[0], DENSITY_FLOOR)
    inverse = reciprocal(density)
    vx, vy, vz = u[1] * inverse, u[2] * inverse, u[3] * inverse
    kinetic = 0.5 * density * (vx * vx + vy * vy + vz * vz)
    energy_b = 0.5 * (u[5] * u[5] + u[6] * u[6] + u[7] * u[7])
    pressure = jnp.maximum((GAMMA - 1.0) * (u[4] - kinetic - energy_b), PRESSURE_FLOOR)
    return [density, vx, vy, vz, pressure, u[5], u[6], u[7]], inverse


def fast_from(sound, alfven, along):
    total = sound + alfven
    inner = jnp.maximum(total * total - 4.0 * sound * along, TINY)
    outer = 0.5 * (total + inner * lax.rsqrt(inner))
    return outer * lax.rsqrt(outer)


def wave(w, n):
    inverse = reciprocal(w[0])
    b2 = w[5] * w[5] + w[6] * w[6] + w[7] * w[7]
    bn = w[5 + n]
    return fast_from(GAMMA * w[4] * inverse, b2 * inverse, bn * bn * inverse), 0.5 * b2


def weighted(w, half_b2, n, weight, shift):
    r, v, p, b = w[0], w[1:4], w[4], w[5:8]
    vn, bn = v[n], b[n]
    k = weight * vn + shift
    q = r * k
    wb = weight * bn
    wp = weight * (p + half_b2)
    energy = p * (1.0 / (GAMMA - 1.0)) + half_b2 + 0.5 * r * (v[0] * v[0] + v[1] * v[1] + v[2] * v[2])
    vb = v[0] * b[0] + v[1] * b[1] + v[2] * b[2]
    momentum = [v[i] * q - b[i] * wb for i in range(3)]
    momentum[n] = momentum[n] + wp
    field = [shift * bn if i == n else b[i] * k - v[i] * wb for i in range(3)]
    return [q] + momentum + [energy * k + wp * vn - wb * vb] + field


def hlle(left, right, n):
    cl, hl = wave(left, n)
    cr, hr = wave(right, n)
    vl, vr = left[1 + n], right[1 + n]
    upper = jnp.maximum(jnp.maximum(vr + cr, vl + cl), 0.0)
    lower = jnp.minimum(jnp.minimum(vl - cl, vr - cr), 0.0)
    inverse = reciprocal(upper - lower)
    a = upper * inverse
    c = a * lower
    first = weighted(left, hl, n, a, -c)
    second = weighted(right, hr, n, -lower * inverse, c)
    return [x + y for x, y in zip(first, second)]


def half_minmod(a, b):
    return 0.5 * (jnp.maximum(jnp.minimum(a, b), 0.0) + jnp.minimum(jnp.maximum(a, b), 0.0))


def roll(x, shift, axis):
    size = x.shape[axis]
    shift = shift % size
    return x if shift == 0 else pltpu.roll(x, shift, axis)


def lane_index():
    return lax.broadcasted_iota(jnp.int32, (8, LANES), 1)


def lane_gather(x, index):
    return jnp.take_along_axis(x, index, axis=1, mode="promise_in_bounds")


def z_up(tiles):
    lane = lane_index()
    edge = lane % BS == 0
    index = lane - lane % BS + (lane + 1) % BS
    moved = [jnp.where(edge, roll(x, -1, 0), x) for x in tiles]
    return jnp.stack([lane_gather(x, index) for x in moved])


def z_down(tiles):
    lane = lane_index()
    edge = lane % BS == BS - 1
    index = lane - lane % BS + (lane + BS - 1) % BS
    moved = [jnp.where(edge, roll(x, 1, 0), x) for x in tiles]
    return jnp.stack([lane_gather(x, index) for x in moved])


def split(x):
    return [x[i] for i in range(x.shape[0])]


def fill_planes(source, w_ref, base):
    def one(c, carry):
        w, _ = primitive([source[c, f] for f in range(FIELDS)])
        for f in range(FIELDS):
            w_ref[base + c, f, 1:YV + 1] = w[f]
        return carry

    lax.fori_loop(0, source.shape[0], one, 0)


def fill_ghosts(glo_ref, ghi_ref, w_ref):
    def one(c, carry):
        for ghost, v, base in ((glo_ref, 0, 96), (ghi_ref, YV + 1, 0)):
            u = [roll(ghost[c, f // 4], base - 32 * (f % 4), 1) for f in range(FIELDS)]
            w, _ = primitive(u)
            for f in range(FIELDS):
                w_ref[c + 2, f, v] = w[f]
        return carry

    lax.fori_loop(0, BS, one, 0)


PAIRS = ((0, 2), (2, 2))


def x_faces(w_ref, sx_ref, fx_ref):
    def slopes(c, carry):
        for f in range(FIELDS):
            here = w_ref[c + 1, f, 1:YV + 1]
            sx_ref[c, f] = half_minmod(
                here - w_ref[c, f, 1:YV + 1], w_ref[c + 2, f, 1:YV + 1] - here
            )
        return carry

    lax.fori_loop(0, BS + 2, slopes, 0)

    def one(face, carry):
        for v, n in PAIRS:
            left = [w_ref[face + 1, f, v + 1:v + 1 + n] + sx_ref[face, f, v:v + n] for f in range(FIELDS)]
            right = [
                w_ref[face + 2, f, v + 1:v + 1 + n] - sx_ref[face + 1, f, v:v + n]
                for f in range(FIELDS)
            ]
            for f, flux in enumerate(hlle(left, right, 0)):
                fx_ref[face, f, v:v + n] = flux
        return carry

    lax.fori_loop(0, BS + 1, one, 0)


def faces(l_ref, r_ref, f_ref, n):
    for v, size in PAIRS:
        left = [l_ref[f, v:v + size] for f in range(FIELDS)]
        right = [r_ref[f, v:v + size] for f in range(FIELDS)]
        for f, flux in enumerate(hlle(left, right, n)):
            f_ref[f, v:v + size] = flux


def y_states(w_ref, c, l_ref, r_ref):
    lane = lax.broadcasted_iota(jnp.int32, (YV + 2, 8, LANES), 2)
    top = lane >= LANES - BS
    bottom = lane < BS
    for f in range(FIELDS):
        w = w_ref[c + 2, f]
        rolled = roll(w, -BS, 2)
        diff = jnp.where(top, jnp.concatenate([rolled[1:], rolled[-1:]]), rolled) - w
        rolled = roll(diff, BS, 2)
        down = jnp.where(bottom, jnp.concatenate([rolled[:1], rolled[:-1]]), rolled)
        slope = half_minmod(down, diff)
        low = roll(w - slope, -BS, 2)
        l_ref[f] = (w + slope)[:YV + 1]
        r_ref[f] = jnp.where(top[1:], low[1:], low[:-1])


def z_states(w_ref, c, l_ref, r_ref):
    for f in range(FIELDS):
        w = w_ref[c + 2, f, 1:YV + 1]
        diff = z_up(split(w)) - w
        slope = half_minmod(z_down(split(diff)), diff)
        l_ref[f] = w + slope
        r_ref[f] = z_up(split(w - slope))


def z_pass(w_ref, acc_ref, lz, rz, fz):
    def two(i, carry):
        for p in range(2):
            z_states(w_ref, 2 * i + p, lz.at[p], rz.at[p])
        for p in range(2):
            faces(lz.at[p], rz.at[p], fz.at[p], 2)
        for p in range(2):
            for f in range(FIELDS):
                flux = fz[p, f]
                acc_ref[2 * i + p, f] = flux - z_down(split(flux))
        return carry

    lax.fori_loop(0, BS // 2, two, 0)


def y_pass(w_ref, acc_ref, ly, ry, fy):
    bottom = lax.broadcasted_iota(jnp.int32, (YV, 8, LANES), 2) < BS

    def two(i, carry):
        for p in range(2):
            y_states(w_ref, 2 * i + p, ly.at[p], ry.at[p])
        left = [jnp.stack([ly[p, f, YV] for p in range(2)]) for f in range(FIELDS)]
        right = [jnp.stack([ry[p, f, YV] for p in range(2)]) for f in range(FIELDS)]
        for f, flux in enumerate(hlle(left, right, 1)):
            for p in range(2):
                fy[p, f, YV] = flux[p]
        for p in range(2):
            faces(ly.at[p], ry.at[p], fy.at[p], 1)
        for p in range(2):
            for f in range(FIELDS):
                flux = fy[p, f]
                rolled = roll(flux, BS, 2)
                across = flux[1:] - jnp.where(bottom, rolled[:-1], rolled[1:])
                acc_ref[2 * i + p, f] = across + acc_ref[2 * i + p, f]
        return carry

    lax.fori_loop(0, BS // 2, two, 0)


def pack(tiles, base):
    group = lane_index() // 32
    out = []
    for q in range(2):
        total = roll(tiles[4 * q], -base, 1)
        for k in range(1, 4):
            total = jnp.where(group == k, roll(tiles[4 * q + k], 32 * k - base, 1), total)
        out.append(total)
    return out


def ring(groups, devs):
    g, j = lax.axis_index("group"), lax.axis_index("dev")
    me = g * devs + j
    count = groups * devs
    after, before = lax.rem(me + 1, count), lax.rem(me + count - 1, count)
    curve_next = (after // devs, lax.rem(after, devs))
    curve_prev = (before // devs, lax.rem(before, devs))
    row = [(g, lax.rem(j + d, devs)) for d in range(1, devs)]
    column = [(lax.rem(g + d, groups), j) for d in range(1, groups)]
    return g, j, me, curve_next, curve_prev, row, column


def greet(peers):
    barrier = pltpu.get_barrier_semaphore()
    for peer in peers:
        pl.semaphore_signal(barrier, inc=1, device_id=peer, device_id_type=MESH)
    pl.semaphore_wait(barrier, len(peers))


def remote(source, target, send, recv, device):
    return pltpu.make_async_remote_copy(
        src_ref=source, dst_ref=target, send_sem=send, recv_sem=recv,
        device_id=device, device_id_type=MESH,
    )


def messages(source, slots, send, recv, peers):
    return [remote(source, slots.at[d], send.at[d], recv.at[d], p) for d, p in enumerate(peers)]


def begin(copies):
    for copy in copies:
        copy.start()


def finish(copies):
    for copy in copies:
        copy.wait()


def step_kernel(
    groups, devs, count_ref, own_ref, flat_ref, out_ref,
    held, flat, outgoing, joined, mine, u_ref, plo, phi,
    count_msg, row_msg, count_row, count_col, total_ref, small_ref, top_ref,
    crow_send, crow_recv, ccol_send, ccol_recv, block_sem, local_sem,
    w_ref, sx_ref, fx_ref, acc_ref, one_ref, edge_lo, edge_hi, plo2, phi2,
    xlo, xhi, glo, ghi, xlo2, xhi2, glo2, ghi2, ly, ry, fy, lz, rz, fz,
    speed_msg, speed_row, speed_col, step_ref,
    row_send, row_recv, col_send, col_recv, send, recv, send2, recv2,
):
    staged = pltpu.make_async_copy(own_ref, held, local_sem.at[0])
    staged.start()
    g, j, me, curve_next, curve_prev, row, column = ring(groups, devs)
    greet(row + column + [curve_next, curve_prev])
    up = (lax.rem(g + 1, groups), j)
    down = (lax.rem(g + groups - 1, groups), j)
    right = (g, lax.rem(j + 1, devs))
    left = (g, lax.rem(j + devs - 1, devs))
    speeds = messages(top_ref, speed_row, row_send, row_recv, row)
    rebalance(
        g, j, me, groups * devs, curve_next, count_ref, own_ref, flat_ref, held, flat, outgoing,
        joined, mine, u_ref, plo, phi, count_msg, row_msg, count_row, count_col, total_ref,
        small_ref, top_ref, row, column, crow_send, crow_recv, ccol_send, ccol_recv, speeds,
        block_sem, local_sem, staged,
    )
    y_copies = [
        remote(phi, glo, send.at[2], recv.at[2], right),
        remote(plo, ghi, send.at[3], recv.at[3], left),
    ]
    begin(y_copies)
    x_copies = [
        remote(u_ref.at[pl.ds(BS - 2, 2)], xlo, send.at[0], recv.at[0], up),
        remote(u_ref.at[pl.ds(0, 2)], xhi, send.at[1], recv.at[1], down),
    ]
    begin(x_copies)

    fill_planes(u_ref, w_ref, 2)
    z_pass(w_ref, acc_ref, lz, rz, fz)

    finish(speeds)
    top = top_ref[...]
    for d in range(devs - 1):
        top = jnp.maximum(top, speed_row[d])
    speed_msg[...] = top
    speeds = messages(speed_msg, speed_col, col_send, col_recv, column)
    begin(speeds)

    finish(y_copies)
    fill_ghosts(glo, ghi, w_ref)
    y_pass(w_ref, acc_ref, ly, ry, fy)
    finish(x_copies)
    fill_planes(xlo, w_ref, 0)
    fill_planes(xhi, w_ref, BS + 2)
    x_faces(w_ref, sx_ref, fx_ref)

    finish(speeds)
    top = speed_msg[...]
    for d in range(groups - 1):
        top = jnp.maximum(top, speed_col[d])
    top = jnp.max(jnp.max(top, axis=1, keepdims=True), axis=0, keepdims=True)
    step_ref[...] = COURANT / jnp.broadcast_to(top, (8, LANES))

    def update(c, edge, place):
        step = step_ref[...]
        low, high = [], []
        for f in range(FIELDS):
            change = (fx_ref[c + 1, f] - fx_ref[c, f]) + acc_ref[c, f]
            new = u_ref[c, f] - step * change
            one_ref[c, f] = new
            if edge is not None:
                edge[place, f] = new
            low.append(new[0])
            high.append(new[YV - 1])
        for q, tile in enumerate(pack(low, 0)):
            plo2[c, q] = tile
        for q, tile in enumerate(pack(high, 96)):
            phi2[c, q] = tile

    def middle(c, carry):
        update(c, None, 0)
        return carry

    for place in range(2):
        update(place, edge_lo, place)
        update(BS - 2 + place, edge_hi, place)
    x_copies = [
        remote(edge_hi, xlo2, send2.at[0], recv2.at[0], up),
        remote(edge_lo, xhi2, send2.at[1], recv2.at[1], down),
    ]
    begin(x_copies)
    lax.fori_loop(2, BS - 2, middle, 0)
    y_copies = [
        remote(phi2, glo2, send2.at[2], recv2.at[2], right),
        remote(plo2, ghi2, send2.at[3], recv2.at[3], left),
    ]
    begin(y_copies)

    fill_planes(one_ref, w_ref, 2)
    z_pass(w_ref, acc_ref, lz, rz, fz)
    finish(y_copies)
    fill_ghosts(glo2, ghi2, w_ref)
    y_pass(w_ref, acc_ref, ly, ry, fy)
    finish(x_copies)
    fill_planes(xlo2, w_ref, 0)
    fill_planes(xhi2, w_ref, BS + 2)
    x_faces(w_ref, sx_ref, fx_ref)

    def last(c, carry):
        step = step_ref[...]
        for f in range(FIELDS):
            change = (fx_ref[c + 1, f] - fx_ref[c, f]) + acc_ref[c, f]
            new = 0.5 * (u_ref[c, f] + one_ref[c, f] - step * change)
            for v in range(YV):
                row = (v // 2) * (BRICK_Z * ROWS) + (c * 2 + v % 2) * FIELDS + f
                out_ref[pl.ds(row, BRICK_Z, stride=ROWS), :] = new[v]
        return carry

    lax.fori_loop(0, BS, last, 0)


def signal_speed(u):
    w, inverse = primitive(u)
    b2 = [w[5 + i] * w[5 + i] for i in range(3)]
    sound = GAMMA * w[4] * inverse
    alfven = (b2[0] + b2[1] + b2[2]) * inverse
    speeds = [jnp.abs(w[1 + i]) + fast_from(sound, alfven, b2[i] * inverse) for i in range(3)]
    return jnp.maximum(jnp.maximum(speeds[0], speeds[1]), speeds[2])


def rebalance(
    g, j, me, total, curve_next, count_ref, own_ref, flat_ref, held, flat, outgoing, joined,
    mine, u_ref, plo, phi, count_msg, row_msg, count_row, count_col, total_ref, small_ref, top_ref,
    row, column, crow_send, crow_recv, ccol_send, ccol_recv, speeds, block_sem, local_sem, staged,
):
    cap = own_ref.shape[0]
    count = count_ref[0]
    count_msg[...] = jnp.full((8, LANES), count, jnp.int32)
    counts = messages(count_msg, count_row, crow_send, crow_recv, row)
    begin(counts)
    staged.wait()

    def stage(m, carry):
        outgoing[m] = held[jnp.clip(count - BLK_DEV + 1 + m, 0, cap - 1)]
        return carry

    lax.fori_loop(0, BLK_DEV - 1, stage, 0)
    blocks = remote(
        outgoing, joined.at[pl.ds(1, BLK_DEV - 1)], block_sem.at[0], block_sem.at[1], curve_next
    )

    @pl.when(me < total - 1)
    def _():
        blocks.start()

    spare = pltpu.make_async_copy(flat_ref, flat, local_sem.at[1])
    spare.start()
    local = pltpu.make_async_copy(
        own_ref.at[pl.ds(0, BLK_DEV)], joined.at[pl.ds(BLK_DEV, BLK_DEV)], local_sem.at[2]
    )
    local.start()

    finish(counts)
    before = jnp.zeros((8, LANES), jnp.int32)
    every = count_msg[...]
    for d in range(1, len(row) + 1):
        value = count_row[d - 1]
        every = every + value
        before = before + jnp.where(d <= j, value, 0)
    row_msg[...] = every
    counts = messages(row_msg, count_col, ccol_send, ccol_recv, column)
    begin(counts)

    spare.wait()
    slot = lax.broadcasted_iota(jnp.int32, (8, LANES), 0)

    def chunk(t, top):
        for first in list(range(0, cap - 8, 8)) + [cap - 8]:
            u = [
                flat[pl.ds(first * ROWS + t * FIELDS + f, 8, stride=ROWS), :]
                for f in range(FIELDS)
            ]
            top = jnp.maximum(top, jnp.where(slot + first < count, signal_speed(u), 0.0))
        return top

    top_ref[...] = lax.fori_loop(0, CHUNKS, chunk, jnp.zeros((8, LANES), jnp.float32))
    begin(speeds)

    finish(counts)
    for d in range(1, len(column) + 1):
        before = before + jnp.where(d <= g, count_col[d - 1], 0)
    total_ref[...] = before - me * BLK_DEV
    narrow = pltpu.make_async_copy(total_ref, small_ref, local_sem.at[3])
    narrow.start()
    narrow.wait()
    surplus = jnp.clip(small_ref[0, 0], 0, BLK_DEV - 1)
    local.wait()

    @pl.when(me < total - 1)
    def _():
        blocks.wait_send()

    @pl.when(me > 0)
    def _():
        blocks.wait_recv()

    def take(k, carry):
        mine[pl.ds(pl.multiple_of(k * ROWS, ROWS), ROWS), :] = joined[BLK_DEV - surplus + k]
        return carry

    lax.fori_loop(0, BLK_DEV, take, 0)

    def assemble(c, carry):
        for v in range(YV):
            for f in range(FIELDS):
                base = (v // 2) * BRICK_Z * ROWS
                u_ref[c, f, v] = mine[
                    pl.ds(base + (c * 2 + v % 2) * FIELDS + f, BRICK_Z, stride=ROWS), :
                ]
        for q, tile in enumerate(pack([u_ref[c, f, 0] for f in range(FIELDS)], 0)):
            plo[c, q] = tile
        for q, tile in enumerate(pack([u_ref[c, f, YV - 1] for f in range(FIELDS)], 96)):
            phi[c, q] = tile
        return carry

    lax.fori_loop(0, BS, assemble, 0)


TILE = (8, LANES)
SLAB = (BS, FIELDS, YV) + TILE
EDGE = (2, FIELDS, YV) + TILE
PACK = (BS, 2) + TILE
LIMIT = 51 * 1024 * 1024


def f32(*shape):
    return jax.ShapeDtypeStruct(shape, jnp.float32)


VMEM = pl.BlockSpec(memory_space=pltpu.VMEM)
ANY = pl.BlockSpec(memory_space=pl.ANY)
SMEM = pl.BlockSpec(memory_space=pltpu.SMEM)


def body(groups, devs, blocks_in, counts):
    cap = blocks_in.shape[0]
    rows = blocks_in.reshape(cap, FIELDS, CHUNKS, LANES).transpose(0, 2, 1, 3)
    rows = rows.reshape(cap, ROWS, LANES)
    dma = pltpu.SemaphoreType.DMA

    def vmem(*shape):
        return pltpu.VMEM(shape, jnp.float32)

    ghosts = [vmem(*EDGE), vmem(*EDGE), vmem(*PACK), vmem(*PACK)]
    out = pl.pallas_call(
        functools.partial(step_kernel, groups, devs),
        out_shape=f32(BLK_DEV * ROWS, LANES),
        in_specs=[SMEM, ANY, ANY],
        out_specs=VMEM,
        scratch_shapes=[
            vmem(cap, ROWS, LANES),
            vmem(cap * ROWS, LANES),
            vmem(BLK_DEV - 1, ROWS, LANES),
            vmem(2 * BLK_DEV, ROWS, LANES),
            vmem(BLK_DEV * ROWS, LANES),
            vmem(*SLAB), vmem(*PACK), vmem(*PACK),
            pltpu.VMEM(TILE, jnp.int32),
            pltpu.VMEM(TILE, jnp.int32),
            pltpu.VMEM((devs - 1,) + TILE, jnp.int32),
            pltpu.VMEM((groups - 1,) + TILE, jnp.int32),
            pltpu.VMEM(TILE, jnp.int32),
            pltpu.SMEM(TILE, jnp.int32),
            vmem(*TILE),
            dma((devs - 1,)), dma((devs - 1,)), dma((groups - 1,)), dma((groups - 1,)),
            dma((2,)), dma((4,)),
            vmem(BS + 4, FIELDS, YV + 2, *TILE),
            vmem(BS + 2, FIELDS, YV, *TILE),
            vmem(BS + 1, FIELDS, YV, *TILE),
            vmem(*SLAB),
            vmem(*SLAB),
        ] + ghosts + ghosts + ghosts + [vmem(2, FIELDS, YV + 1, *TILE)] * 3
        + [vmem(2, FIELDS, YV, *TILE)] * 3 + [
            vmem(*TILE), vmem(devs - 1, *TILE), vmem(groups - 1, *TILE), vmem(*TILE),
            dma((devs - 1,)), dma((devs - 1,)), dma((groups - 1,)), dma((groups - 1,)),
            dma((4,)), dma((4,)), dma((4,)), dma((4,)),
        ],
        compiler_params=pltpu.CompilerParams(
            collective_id=0, has_side_effects=True, vmem_limit_bytes=LIMIT
        ),
        name="step",
    )(counts, rows, rows.reshape(cap * ROWS, LANES))
    out = out.reshape(BLK_DEV, CHUNKS, FIELDS, LANES).transpose(0, 2, 1, 3)
    return out.reshape(BLK_DEV, FIELDS, CHUNKS * LANES)


def solution(mesh):
    groups, devs = mesh.shape["group"], mesh.shape["dev"]
    in_specs = (P(("group", "dev"), None, None), P(("group", "dev")))
    out_specs = P(("group", "dev"), None, None)
    return jax.shard_map(
        functools.partial(body, groups, devs),
        mesh=mesh, in_specs=in_specs, out_specs=out_specs, check_vma=False,
    )
```
